32 devices in a mesh: node: 4 (over y, core), local: 8 (over z, x).
Axes of the slice: x: 2, y: 2, z: 4, core: 2. Of those that a mesh axis runs over, the one named last changes fastest.
Arguments:
- tokens: bfloat16 [4096, 2048], P(('node', 'local')), may hold values from -6 to 6
- cotangent: bfloat16 [4096, 2048], P(('node', 'local')), may hold values from -6 to 6
- routes: int32 [4096, 1], P('node'), may hold values from 0 to 3; in each aligned block of 1024 rows (0 to 1023, 1024 to 2047, ...) at most 272 rows name the same one
- route_weight: float32 [4096, 1], P('node'), may hold values from 0.2 to 1
- fetch_pick: int32 [4, 4], replicated, may hold values from 0 to 1
- panels: bfloat16 [8, 3, 1408, 2048], P('node', None, 'local'), may hold values from -0.125 to 0.125
Outputs:
- mixed: bfloat16 [4096, 2048], P(('node', 'local'))
- token_grad: bfloat16 [4096, 2048], P(('node', 'local'))
- panel_grad: bfloat16 [8, 3, 1408, 2048], P('node', None, 'local')
The draws below stay inside these ranges and needn't reach their ends.
Inputs may be any that keep to these rules, and one draw needn't show every extreme that they name: `routes`: each row names 1 different slots; in the 1024 rows of one group no slot is named by more than 272 rows, and in some groups one slot is named by exactly 272 rows.
All inputs are finite; a program needn't handle non-finite values.
Results may differ from the reference program's by a relative error of at most 0.013.
Values may be sent and summed in bfloat16 or wider, within the bound.
No kernel may reach another device: no remote copies, remote signals or barrier semaphores. Data moves between devices by JAX's collectives and lax.ppermute only.
A program may use at most 128 MiB of HBM per device.

```python
import math
import jax
import jax.numpy as jnp
import numpy as np
from jax import lax

D = 2048
FF = 1408
EXP_NODE = 2
SLOTS = 4
TOPK = 1
TOKENS = 4096
GROUP = 1024
EXPERTS = 8
CAP = 272
N_NODE = 4
N_LOCAL = 8


def with_ends(values, stream_key, least, largest):
    dims = values.shape
    index_at = [jax.random.randint(jax.random.fold_in(stream_key, axis), (), 0, dims[axis]) for axis in range(len(dims))]
    values = values.at[tuple(index_at)].set(least)
    longest = dims.index(max(dims))
    index_at[longest] = (index_at[longest] + 1) % dims[longest]
    return values.at[tuple(index_at)].set(largest)


def steps_of(stream_key, shape, shards, smallest, top_value):
    def one(dim, parts):
        steps = jax.random.uniform(jax.random.fold_in(jax.random.fold_in(stream_key, 6), dim), (parts,), jnp.float32, smallest / len(shards), top_value / len(shards))
        return jnp.repeat(jnp.exp(steps), shape[dim] // parts).reshape((-1,) + (1,) * (len(shape) - dim - 1))

    loudness = one(*shards[0])
    for cut in shards[1:]:
        loudness = loudness * one(*cut)
    return loudness


def routed_block(own_key, own, number, rows, number_of, top, limit, skew):
    sequence = jax.random.permutation(own_key, number_of)
    packed, usual = load_shares(number_of, rows * top, limit, skew, True), load_shares(number_of, rows * top, limit, skew, False)
    places = jnp.arange(number_of)

    def named(tallies, offset_by):
        used = int((tallies > 0).sum())
        fixed = max(1, used // 4)
        passed = fixed + (places - fixed + offset_by * (used - fixed)) % max(1, number_of - fixed)
        return jnp.zeros((number_of,), jnp.int32).at[sequence[jnp.where(places < fixed, places, passed)]].set(jnp.asarray(tallies, jnp.int32))

    tallies = jnp.where(number % 4 == 0, named(packed, number // 4), named(usual, number - number // 4 - 1))
    mixed = jax.random.permutation(jax.random.fold_in(own, 3), number_of)
    giver, receiver = mixed[0:number_of // 2 * 2:2], mixed[1:number_of // 2 * 2:2]
    margin = jnp.minimum(tallies[giver] - 1, limit - tallies[receiver]) // 2
    margin = jnp.where((giver == sequence[0]) | (receiver == sequence[0]) | (tallies[receiver] == 0), 0, jnp.maximum(margin, 0))
    passed = jax.random.randint(jax.random.fold_in(own, 4), (number_of // 2,), 0, 1 << 20) % (margin + 1)
    tallies = tallies.at[giver].add(-passed).at[receiver].add(passed)
    members = jnp.searchsorted(jnp.cumsum(tallies), jnp.arange(rows * top), side="right").astype(jnp.int32)
    table = members.reshape(top, rows).T
    table = table[jax.random.permutation(jax.random.fold_in(own, 1), rows)]
    offset_by = jax.random.randint(jax.random.fold_in(own, 2), (rows, 1), 0, top)
    return jnp.take_along_axis(table, (jnp.arange(top)[None, :] + offset_by) % top, axis=1)


def load_shares(amount, total, limit, slope, full):
    loads = [(1 << 20) // math.isqrt(grade ** slope) + 1 for grade in range(1, amount + 1)]
    largest = limit if full else min(limit, max(-(-total // amount), total * loads[0] // sum(loads)))
    least = 1 if total - largest >= amount - 1 else 0
    holding, surplus = [largest] + [least] * (amount - 1), total - largest - least * (amount - 1)
    while surplus > 0:
        movable = [i for i in range(1, amount) if holding[i] < largest] or [i for i in range(1, amount) if holding[i] < limit]
        mass, remaining = sum([loads[i] for i in movable]), surplus
        for i in movable:
            more = min(limit - holding[i], max(1, remaining * loads[i] // mass), surplus)
            holding[i] = holding[i] + more
            surplus = surplus - more
    return np.array(holding)


def scatter_about(own_key, shape, spread, reach, split=(), kind=jnp.bfloat16):
    gain = steps_of(own_key, shape, split, -0.22, 0.18) if split else 1.0
    drawn = jax.random.normal(own_key, shape, jnp.float32) * spread * gain
    return jnp.minimum(jnp.maximum(drawn, -reach), reach).astype(kind)


def setup_inputs(seed: int = 0) -> dict:
    seeds = jax.random.split(jax.random.key(seed), 7)
    tokens = scatter_about(seeds[0], (TOKENS, D), 1.0, 6.0, ((0, 32),))
    cotangent = scatter_about(seeds[1], (TOKENS, D), 1.0, 6.0, ((0, 32),))
    routes_keys = jax.random.split(jax.random.fold_in(seeds[2], 1), TOKENS // GROUP)
    routes_turns = jax.random.permutation(jax.random.fold_in(seeds[2], 3), TOKENS // GROUP)
    routes = jax.vmap(lambda own, number: routed_block(jax.random.fold_in(seeds[2], 2), own, number, GROUP, SLOTS, TOPK, CAP, 1))(routes_keys, routes_turns).reshape((TOKENS, TOPK))
    route_weight = jnp.clip(jnp.exp(math.log(1.0) - 1.609438 * jax.random.uniform(seeds[3], (TOKENS, TOPK), jnp.float32) ** steps_of(seeds[3], (TOKENS, TOPK), ((0, 4),), -0.2, 0.2)), 0.2, 1.0)
    fetch_pick = with_ends(jax.random.randint(seeds[4], (N_NODE, SLOTS), 0, EXP_NODE), jax.random.fold_in(seeds[4], 1), 0, EXP_NODE - 1).astype(jnp.int32)
    panels = scatter_about(seeds[5], (EXPERTS, 3, FF, D), D ** -0.5, 0.125, ((0, 4), (2, 8)))
    return {"tokens": tokens, "cotangent": cotangent, "routes": routes, "route_weight": route_weight, "fetch_pick": fetch_pick, "panels": panels}


def silu_parts(gate_pre):
    sigmoid_gate = jax.nn.sigmoid(gate_pre)
    return gate_pre * sigmoid_gate, sigmoid_gate


def dispatch_table(group_routes, group_weight, slot_count, capacity, group_size):
    route_count = group_routes.shape[1]
    flat_slot = group_routes.reshape(-1).astype(jnp.int32)
    onehot = (flat_slot[:, None] == jnp.arange(slot_count, dtype=jnp.int32)[None, :]).astype(jnp.int32)
    position = jnp.sum((jnp.cumsum(onehot, axis=0) - 1) * onehot, axis=1)
    target = (flat_slot * capacity + position).astype(jnp.int32)
    token_ids = (jnp.arange(group_size * route_count, dtype=jnp.int32) // route_count).astype(jnp.int32)
    source = jnp.full((slot_count * capacity,), group_size, jnp.int32).at[target].set(token_ids)
    slot_weight = jnp.zeros((slot_count * capacity,), group_weight.dtype).at[target].set(group_weight.reshape(-1))
    return target, source, slot_weight


def reference(tokens, cotangent, routes, route_weight, fetch_pick, panels):
    stride = N_NODE // SLOTS
    slice_width = FF // N_LOCAL
    group_tokens = tokens.reshape(N_NODE, GROUP, D)
    group_cotan = cotangent.reshape(N_NODE, GROUP, D)
    group_routes = routes.reshape(N_NODE, GROUP, TOPK)
    group_weights = route_weight.reshape(N_NODE, GROUP, TOPK)
    node_ids = jnp.arange(N_NODE, dtype=jnp.int32)

    def split_rows(values):
        return values.reshape(CAP, N_LOCAL, slice_width).astype(jnp.float32)

    def split_panel(matrix):
        return matrix.reshape(N_LOCAL, slice_width, D).astype(jnp.float32)

    def one_group(accumulated, inputs):
        node_index, group_x, group_dy, slot_routes, slot_weights = inputs
        target, source, slot_weight = dispatch_table(slot_routes, slot_weights, SLOTS, CAP, GROUP)
        zero_row = jnp.zeros((1, D), group_x.dtype)
        slot_tokens = jnp.concatenate([group_x, zero_row], axis=0)[source].reshape(SLOTS, CAP, D)
        slot_dy = jnp.concatenate([group_dy, zero_row], axis=0)[source].reshape(SLOTS, CAP, D)
        slot_cotan = (slot_dy.astype(jnp.float32) * slot_weight.reshape(SLOTS, CAP, 1)).astype(jnp.bfloat16)
        expert_outs = []
        input_grads = []
        for round_index in range(SLOTS):
            owner = (node_index - round_index * stride) % N_NODE
            expert = (owner * EXP_NODE + fetch_pick[node_index, round_index]).astype(jnp.int32)
            panel = lax.dynamic_index_in_dim(panels, expert, 0, keepdims=False)
            rows_in = slot_tokens[round_index]
            rows_cotan = slot_cotan[round_index]
            gate_pre = jnp.dot(rows_in, panel[0].T, preferred_element_type=jnp.float32)
            up_pre = jnp.dot(rows_in, panel[1].T, preferred_element_type=jnp.float32)
            activated, sigmoid_gate = silu_parts(gate_pre)
            hidden = (activated * up_pre).astype(jnp.bfloat16)
            d_hidden = jnp.dot(rows_cotan, panel[2].T, preferred_element_type=jnp.float32)
            d_gate = (d_hidden * up_pre * sigmoid_gate * (1.0 + gate_pre * (1.0 - sigmoid_gate))).astype(jnp.bfloat16)
            d_up = (d_hidden * activated).astype(jnp.bfloat16)
            expert_outs.append(jnp.einsum("cla,lad->lcd", split_rows(hidden), split_panel(panel[2])))
            input_grads.append(jnp.einsum("cla,lad->lcd", split_rows(d_gate), split_panel(panel[0]))
                               + jnp.einsum("cla,lad->lcd", split_rows(d_up), split_panel(panel[1])))
            weight_grad = jnp.stack([
                jnp.dot(d_gate.T, rows_in, preferred_element_type=jnp.float32),
                jnp.dot(d_up.T, rows_in, preferred_element_type=jnp.float32),
                jnp.dot(hidden.T, rows_cotan, preferred_element_type=jnp.float32)]).astype(jnp.bfloat16)
            accumulated = accumulated.at[expert].add(weight_grad.astype(jnp.float32))
        out_all = jnp.concatenate(expert_outs, axis=1)
        grad_all = jnp.concatenate(input_grads, axis=1)
        picked_out = out_all[:, target].reshape(N_LOCAL, GROUP, TOPK, D)
        mixed_parts = jnp.sum(picked_out * slot_weights[None, :, :, None], axis=2).astype(jnp.bfloat16)
        mixed_group = jnp.sum(mixed_parts.astype(jnp.float32), axis=0).astype(jnp.bfloat16)
        picked_grad = grad_all[:, target].reshape(N_LOCAL, GROUP, TOPK, D)
        grad_parts = jnp.sum(picked_grad, axis=2).astype(jnp.bfloat16)
        grad_group = jnp.sum(grad_parts.astype(jnp.float32), axis=0).astype(jnp.bfloat16)
        return accumulated, (mixed_group, grad_group)

    start = jnp.zeros((EXPERTS, 3, FF, D), jnp.float32)
    accumulated, (mixed, token_grad) = lax.scan(
        one_group, start, (node_ids, group_tokens, group_cotan, group_routes, group_weights))
    return (mixed.reshape(TOKENS, D), token_grad.reshape(TOKENS, D), accumulated.astype(jnp.bfloat16))
```

```python
import jax
import jax.numpy as jnp
from jax import lax
from jax.experimental import pallas as pl
from jax.experimental.pallas import tpu as pltpu
from jax.sharding import PartitionSpec as P

BF16 = jnp.bfloat16
F32 = jnp.float32
VMEM_LIMIT = 48 * 1024 * 1024
CONTRACT_LAST = (((1,), (1,)), ((), ()))
CONTRACT_FIRST = (((0,), (0,)), ((), ()))


def whole_in_vmem():
    return pl.BlockSpec(memory_space=pltpu.VMEM)


def tile_of(size, most):
    tile = min(size, most)
    while size % tile:
        tile -= 1
    return tile


def from_behind(block, axis, distance):
    size = lax.axis_size(axis)
    return lax.ppermute(block, axis, [((i - distance) % size, i) for i in range(size)])


def ring_order(size):
    return list(range(0, size, 2)) + list(range(1, size, 2))[::-1]


def ring_step(block, order, distance):
    size = len(order)
    return lax.ppermute(
        block, "local", [(order[i], order[(i + distance) % size]) for i in range(size)]
    )


def ring_gather(block, order, up_hops):
    size = len(order)
    blocks = [block] + [None] * (size - 1)
    up, down = block, block
    for hop in range(1, max(up_hops, size - 1 - up_hops) + 1):
        if hop <= up_hops:
            up = ring_step(up, order, 1)
            blocks[size - hop] = up
        if hop <= size - 1 - up_hops:
            down = ring_step(down, order, -1)
            blocks[hop] = down
    return blocks


def plus(a, b):
    return (a.astype(F32) + b.astype(F32)).astype(BF16)


def ring_scatter(chunks, order, up_hops):
    size = len(order)
    down_hops = size - 1 - up_hops
    up, down = chunks[up_hops], chunks[(size - down_hops) % size]
    for hop in range(max(up_hops, down_hops), 0, -1):
        if hop <= up_hops:
            up = ring_step(up, order, 1)
            if hop > 1:
                up = plus(up, chunks[hop - 1])
        if hop <= down_hops:
            down = ring_step(down, order, -1)
            if hop > 1:
                down = plus(down, chunks[size - hop + 1])
    return (up.astype(F32) + down.astype(F32) + chunks[0].astype(F32)).astype(BF16)


def slot_kernel(slot, parts, *refs):
    x_refs, dy_refs = refs[:parts], refs[parts : 2 * parts]
    panel, routes, weight, acts, grads = refs[2 * parts : 2 * parts + 5]
    x_all, dy_all = refs[2 * parts + 5 :]
    units = panel.shape[1]
    part, width = x_refs[0].shape
    for d in range(parts):
        x_all[d * part : (d + 1) * part, :] = x_refs[d][...]
        dy_all[d * part : (d + 1) * part, :] = dy_refs[d][...]
    rows = tile_of(x_all.shape[0], 256)
    columns = tile_of(width, 512)

    @pl.loop(0, x_all.shape[0] // rows)
    def _(step):
        here = pl.ds(pl.multiple_of(step * rows, rows), rows)
        x, dy = x_all[here, :], dy_all[here, :]
        gate = lax.dot_general(panel[0], x, CONTRACT_LAST, preferred_element_type=F32)
        up = lax.dot_general(panel[1], x, CONTRACT_LAST, preferred_element_type=F32)
        d_hidden = lax.dot_general(panel[2], dy, CONTRACT_LAST, preferred_element_type=F32)
        scale = jnp.where(routes[:, here] == slot, weight[:, here], 0.0)
        sigmoid_gate = jax.nn.sigmoid(gate)
        activated = gate * sigmoid_gate
        d_hidden = d_hidden * scale
        d_gate = d_hidden * up * sigmoid_gate * (1.0 + gate * (1.0 - sigmoid_gate))
        acts[0:units, here] = d_gate.astype(BF16)
        acts[units : 2 * units, here] = (d_hidden * activated).astype(BF16)
        acts[2 * units : 3 * units, here] = (activated * up * scale).astype(BF16)

    @pl.loop(0, width // columns)
    def _(step):
        here = pl.ds(pl.multiple_of(step * columns, columns), columns)
        x, dy = x_all[:, here], dy_all[:, here]
        d_both = jnp.dot(acts[0 : 2 * units, :], x, preferred_element_type=F32).astype(BF16)
        grads[0, :, here] = d_both[0:units]
        grads[1, :, here] = d_both[units:]
        grads[2, :, here] = jnp.dot(
            acts[2 * units : 3 * units, :], dy, preferred_element_type=F32
        ).astype(BF16)


def slot_pass(slot, x_parts, dy_parts, panel, routes, weight):
    parts = len(x_parts)
    part, width = x_parts[0].shape
    units = panel.shape[1]
    total = parts * part
    return pl.pallas_call(
        lambda *refs: slot_kernel(slot, parts, *refs),
        out_shape=(
            jax.ShapeDtypeStruct((3 * units, total), BF16),
            jax.ShapeDtypeStruct(panel.shape, BF16),
        ),
        in_specs=[whole_in_vmem()] * (2 * parts + 3),
        out_specs=(whole_in_vmem(), whole_in_vmem()),
        scratch_shapes=[pltpu.VMEM((total, width), BF16), pltpu.VMEM((total, width), BF16)],
        compiler_params=pltpu.CompilerParams(vmem_limit_bytes=VMEM_LIMIT),
        cost_estimate=pl.CostEstimate(
            flops=12 * total * units * width,
            bytes_accessed=4 * total * width + 12 * units * width,
            transcendentals=total * units,
        ),
        name=f"slot_{slot}",
    )(*x_parts, *dy_parts, panel, routes, weight)


def chunk_kernel(wanted, slots, part, *refs):
    acts, panels, outs = refs[:slots], refs[slots : 2 * slots], refs[2 * slots :]
    units, width = panels[0].shape[1:]
    columns = tile_of(width, 512)

    @pl.loop(0, width // columns)
    def _(step):
        here = pl.ds(pl.multiple_of(step * columns, columns), columns)
        for out, (kind, d) in zip(outs, wanted):
            rows = slice(d * part, (d + 1) * part)
            total = jnp.zeros((part, columns), F32)
            for act, panel in zip(acts, panels):
                for which in (2,) if kind == "mixed" else (0, 1):
                    total += lax.dot_general(
                        act[which * units : (which + 1) * units, rows],
                        panel[which, :, here],
                        CONTRACT_FIRST,
                        preferred_element_type=F32,
                    )
            out[:, here] = total.astype(BF16)


def chunk_pass(wanted, acts, panels, part):
    slots = len(acts)
    units, width = panels[0].shape[1:]
    work = sum(1 if kind == "mixed" else 2 for kind, _ in wanted)
    return pl.pallas_call(
        lambda *refs: chunk_kernel(wanted, slots, part, *refs),
        out_shape=tuple(jax.ShapeDtypeStruct((part, width), BF16) for _ in wanted),
        in_specs=[whole_in_vmem()] * (2 * slots),
        out_specs=tuple(whole_in_vmem() for _ in wanted),
        compiler_params=pltpu.CompilerParams(vmem_limit_bytes=VMEM_LIMIT),
        cost_estimate=pl.CostEstimate(
            flops=2 * work * slots * part * units * width,
            bytes_accessed=slots * 6 * units * width + 2 * len(wanted) * part * width,
            transcendentals=0,
        ),
        name=f"chunks_{len(wanted)}",
    )(*acts, *panels)


def body(tokens, cotangent, routes, route_weight, fetch_pick, panels):
    node_count = lax.axis_size("node")
    my_node = lax.axis_index("node")
    my_local = lax.axis_index("local")
    slot_count = fetch_pick.shape[1]
    stride = node_count // slot_count
    part, width = tokens.shape
    order = ring_order(lax.axis_size("local"))
    size = len(order)

    x_parts = ring_gather(tokens, order, size // 2)
    dy_parts = ring_gather(cotangent, order, size - 1 - size // 2)

    place = jnp.asarray([order.index(i) for i in range(size)], jnp.int32)[my_local]
    sources = jnp.asarray(order + order, jnp.int32)
    sources = lax.dynamic_slice(sources, (place,), (size,))
    ring_routes = routes.reshape(size, part)[sources].reshape(1, size * part)
    ring_weight = route_weight.reshape(size, part)[sources].reshape(1, size * part)

    def chosen_local(round_index):
        reader = (my_node + round_index * stride) % node_count
        return fetch_pick[reader, round_index]

    chosen = [chosen_local(r) for r in range(slot_count)]
    read = []
    for r in range(slot_count):
        panel = lax.dynamic_index_in_dim(panels, chosen[r], 0, keepdims=False)
        read.append(from_behind(panel, "node", r * stride) if r else panel)

    acts, grads = [None] * slot_count, [None] * slot_count
    for r in list(range(1, slot_count)) + [0]:
        acts[r], grad = slot_pass(r, x_parts, dy_parts, read[r], ring_routes, ring_weight)
        grads[r] = from_behind(grad, "node", node_count - r * stride) if r else grad

    first = size // 2
    early = [("mixed", first), ("grad", size - 1 - first), ("mixed", first + 1), ("grad", first)]
    late = [
        (kind, d)
        for hop in range(first, -1, -1)
        for d in {hop: 0, size - hop: 0}
        if d < size
        for kind in ("mixed", "grad")
        if (kind, d) not in early
    ]
    done = dict(zip(early, chunk_pass(early, acts, read, part)))
    done.update(zip(late, chunk_pass(late, acts, read, part)))
    mixed = ring_scatter([done["mixed", d] for d in range(size)], order, size // 2)
    token_grad = ring_scatter([done["grad", d] for d in range(size)], order, size - 1 - size // 2)

    panel_grad = jnp.stack(
        [
            sum(jnp.where(chosen[r] == e, grads[r].astype(F32), 0.0) for r in range(slot_count))
            for e in range(panels.shape[0])
        ]
    ).astype(BF16)
    return mixed, token_grad, panel_grad


def solution(mesh):
    return jax.shard_map(
        body,
        mesh=mesh,
        in_specs=(
            P(("node", "local"), None),
            P(("node", "local"), None),
            P("node", None),
            P("node", None),
            P(),
            P("node", None, "local", None),
        ),
        out_specs=(
            P(("node", "local"), None),
            P(("node", "local"), None),
            P("node", None, "local", None),
        ),
        check_vma=False,
    )
```

```python
import jax
import jax.numpy as jnp
from jax import lax
from jax.experimental import pallas as pl
from jax.experimental.pallas import tpu as pltpu
from jax.sharding import PartitionSpec as P

BF16 = jnp.bfloat16
F32 = jnp.float32
VMEM_LIMIT = 24 * 1024 * 1024
CONTRACT_LAST = (((1,), (1,)), ((), ()))
CONTRACT_FIRST = (((0,), (0,)), ((), ()))


def whole_in_vmem():
    return pl.BlockSpec(memory_space=pltpu.VMEM)


def untouched():
    return pl.BlockSpec(memory_space=pl.ANY)


def tile_of(size, most):
    tile = min(size, most)
    while size % tile:
        tile -= 1
    return tile


def from_behind(block, axis, distance):
    size = lax.axis_size(axis)
    return lax.ppermute(block, axis, [((i - distance) % size, i) for i in range(size)])


def ring_order(size):
    return list(range(0, size, 2)) + list(range(1, size, 2))[::-1]


def ring_source(size, ahead):
    me = lax.axis_index("local")
    half = lax.div(size + 1, 2)
    place = jnp.where(lax.rem(me, 2) == 0, lax.div(me, 2), size - 1 - lax.div(me, 2))
    there = lax.rem(place + ahead, size)
    return jnp.where(there < half, 2 * there, 2 * (size - 1 - there) + 1)


def chosen_of(fetch_pick, slot, node_count):
    stride = node_count // fetch_pick.shape[1]
    return fetch_pick[lax.rem(lax.axis_index("node") + slot * stride, node_count), slot]


def pick_kernel(slots, node_count, fetch_pick, panels, *refs):
    outs, sems = refs[: len(slots)], refs[len(slots)]
    copies = [
        pltpu.make_async_copy(panels.at[chosen_of(fetch_pick, slot, node_count)], out, sems.at[i])
        for i, (slot, out) in enumerate(zip(slots, outs))
    ]
    for copy in copies:
        copy.start()
    for copy in copies:
        copy.wait()


def pick_pass(slots, node_count, fetch_pick, panels):
    return pl.pallas_call(
        lambda *refs: pick_kernel(slots, node_count, *refs),
        out_shape=tuple(jax.ShapeDtypeStruct(panels.shape[1:], BF16) for _ in slots),
        in_specs=[pl.BlockSpec(memory_space=pltpu.SMEM), untouched()],
        out_specs=tuple(untouched() for _ in slots),
        scratch_shapes=[pltpu.SemaphoreType.DMA((len(slots),))],
        compiler_params=pltpu.CompilerParams(vmem_limit_bytes=VMEM_LIMIT),
        name="pick",
    )(fetch_pick, panels)


def total_kernel(node_count, fetch_pick, *refs):
    grads, out = refs[:-1], refs[-1]
    chosen = [chosen_of(fetch_pick, slot, node_count) for slot in range(len(grads))]
    for e in range(out.shape[0]):
        total = jnp.zeros(grads[0].shape, F32)
        for pick, grad in zip(chosen, grads):
            total += jnp.where(pick == e, grad[...].astype(F32), 0.0)
        out[e] = total.astype(BF16)


def total_pass(node_count, fetch_pick, grads, shape):
    kinds, units, width = grads[0].shape
    block = pl.BlockSpec((1, units, width), lambda i: (i, 0, 0))
    return pl.pallas_call(
        lambda *refs: total_kernel(node_count, *refs),
        out_shape=jax.ShapeDtypeStruct(shape, BF16),
        grid=(kinds,),
        in_specs=[pl.BlockSpec(memory_space=pltpu.SMEM)] + [block] * len(grads),
        out_specs=pl.BlockSpec((shape[0], 1, units, width), lambda i: (0, i, 0, 0)),
        compiler_params=pltpu.CompilerParams(vmem_limit_bytes=VMEM_LIMIT),
        name="total",
    )(fetch_pick, *grads)


def ring_step(block, order, distance):
    size = len(order)
    return lax.ppermute(
        block, "local", [(order[i], order[(i + distance) % size]) for i in range(size)]
    )


def ring_gather(block, order, up_hops):
    size = len(order)
    blocks = [block] + [None] * (size - 1)
    up, down = block, block
    for hop in range(1, max(up_hops, size - 1 - up_hops) + 1):
        if hop <= up_hops:
            up = ring_step(up, order, 1)
            blocks[size - hop] = up
        if hop <= size - 1 - up_hops:
            down = ring_step(down, order, -1)
            blocks[hop] = down
    return blocks


def plus(a, b):
    return (a.astype(F32) + b.astype(F32)).astype(BF16)


def ring_scatter(chunks, order, up_hops):
    size = len(order)
    down_hops = size - 1 - up_hops
    up, down = chunks[up_hops], chunks[(size - down_hops) % size]
    for hop in range(max(up_hops, down_hops), 0, -1):
        if hop <= up_hops:
            up = ring_step(up, order, 1)
            if hop > 1:
                up = plus(up, chunks[hop - 1])
        if hop <= down_hops:
            down = ring_step(down, order, -1)
            if hop > 1:
                down = plus(down, chunks[size - hop + 1])
    return (up.astype(F32) + down.astype(F32) + chunks[0].astype(F32)).astype(BF16)


def acts_kernel(slot, size, offsets, *refs):
    parts = len(offsets)
    x_refs, dy_refs = refs[:parts], refs[parts : 2 * parts]
    panel, routes, weight, acts = *refs[2 * parts : 2 * parts + 3], refs[-1]
    units, width = panel.shape[1:]
    part = x_refs[0].shape[0]
    at_once = 2 if parts % 2 == 0 else 1
    for d in range(0, parts, at_once):
        here = slice(d * part, (d + at_once) * part)
        x = jnp.concatenate([ref[...] for ref in x_refs[d : d + at_once]], axis=0)
        dy = jnp.concatenate([ref[...] for ref in dy_refs[d : d + at_once]], axis=0)
        both = lax.dot_general(
            panel[0:2].reshape(2 * units, width), x, CONTRACT_LAST, preferred_element_type=F32
        )
        gate, up = both[:units], both[units:]
        d_hidden = lax.dot_general(panel[2], dy, CONTRACT_LAST, preferred_element_type=F32)
        sources = [ring_source(size, ahead) for ahead in offsets[d : d + at_once]]
        scale = jnp.concatenate(
            [
                jnp.where(routes[pl.ds(i, 1), :] == slot, weight[pl.ds(i, 1), :], 0.0)
                for i in sources
            ],
            axis=1,
        )
        sigmoid_gate = jax.nn.sigmoid(gate)
        activated = gate * sigmoid_gate
        d_hidden = d_hidden * scale
        d_gate = d_hidden * up * sigmoid_gate * (1.0 + gate * (1.0 - sigmoid_gate))
        acts[0:units, here] = d_gate.astype(BF16)
        acts[units : 2 * units, here] = (d_hidden * activated).astype(BF16)
        acts[2 * units : 3 * units, here] = (activated * up * scale).astype(BF16)


def acts_pass(name, slot, offsets, x_parts, dy_parts, panel, routes, weight, after=()):
    parts = len(x_parts)
    part = x_parts[0].shape[0]
    return pl.pallas_call(
        lambda *refs: acts_kernel(slot, routes.shape[0], offsets, *refs),
        out_shape=jax.ShapeDtypeStruct((3 * panel.shape[1], parts * part), BF16),
        in_specs=[whole_in_vmem()] * (2 * parts + 3) + [untouched()] * len(after),
        out_specs=whole_in_vmem(),
        compiler_params=pltpu.CompilerParams(vmem_limit_bytes=VMEM_LIMIT),
        name=f"acts_{slot}_{name}",
    )(*x_parts, *dy_parts, panel, routes, weight, *after)


def grads_kernel(parts, groups, *refs):
    x_refs, dy_refs = refs[:parts], refs[parts : 2 * parts]
    acts, grads = refs[2 * parts : 2 * parts + groups], refs[-1]
    units, width = grads.shape[1:]
    columns = tile_of(width, 512)
    for start in range(0, width, columns):
        here = slice(start, start + columns)
        x = jnp.concatenate([ref[:, here] for ref in x_refs], axis=0)
        dy = jnp.concatenate([ref[:, here] for ref in dy_refs], axis=0)
        d_both = jnp.concatenate([act[0 : 2 * units, :] for act in acts], axis=1)
        d_both = jnp.dot(d_both, x, preferred_element_type=F32).astype(BF16)
        grads[0, :, here] = d_both[0:units]
        grads[1, :, here] = d_both[units:]
        hidden = jnp.concatenate([act[2 * units : 3 * units, :] for act in acts], axis=1)
        grads[2, :, here] = jnp.dot(hidden, dy, preferred_element_type=F32).astype(BF16)


def grads_pass(slot, x_parts, dy_parts, acts, shape, after=()):
    parts = len(x_parts)
    return pl.pallas_call(
        lambda *refs: grads_kernel(parts, len(acts), *refs),
        out_shape=jax.ShapeDtypeStruct(shape, BF16),
        in_specs=[whole_in_vmem()] * (2 * parts + len(acts)) + [untouched()] * len(after),
        out_specs=whole_in_vmem(),
        compiler_params=pltpu.CompilerParams(vmem_limit_bytes=VMEM_LIMIT),
        name=f"grads_{slot}",
    )(*x_parts, *dy_parts, *acts, *after)


def chunk_kernel(wanted, slots, part, acts, panels, outs):
    units, width = panels[0].shape[1:]
    columns = tile_of(width, 512)

    @pl.loop(0, width // columns)
    def _(step):
        here = pl.ds(pl.multiple_of(step * columns, columns), columns)
        kinds = {"mixed": (2, 3), "grad": (0, 2)}
        sides = {
            kind: jnp.concatenate(
                [panel[which, :, here] for panel in panels for which in range(*span)], axis=0
            )
            for kind, span in kinds.items()
        }
        for out, (kind, group, row) in zip(outs, wanted):
            low, high = (units * which for which in kinds[kind])
            act = jnp.concatenate(
                [act[group][low:high, row * part : (row + 1) * part] for act in acts], axis=0
            )
            total = lax.dot_general(act, sides[kind], CONTRACT_FIRST, preferred_element_type=F32)
            out[:, here] = total.astype(BF16)


def chunk_pass(wanted, acts, panels, groups, part, after=()):
    slots = len(panels)
    width = panels[0].shape[2]
    named = [
        (kind, g, group.index(d)) for kind, d in wanted for g, group in enumerate(groups) if d in group
    ]

    def kernel(*refs):
        act_refs = [refs[s * len(groups) : (s + 1) * len(groups)] for s in range(slots)]
        rest = refs[slots * len(groups) :]
        chunk_kernel(named, slots, part, act_refs, rest[:slots], rest[slots + len(after) :])

    return pl.pallas_call(
        kernel,
        out_shape=tuple(jax.ShapeDtypeStruct((part, width), BF16) for _ in wanted),
        in_specs=[whole_in_vmem()] * (slots * len(groups) + slots) + [untouched()] * len(after),
        out_specs=tuple(whole_in_vmem() for _ in wanted),
        compiler_params=pltpu.CompilerParams(vmem_limit_bytes=VMEM_LIMIT),
        name=f"chunks_{len(wanted)}",
    )(*[act for slot_acts in acts for act in slot_acts], *panels, *after)


def body(tokens, cotangent, routes, route_weight, fetch_pick, panels):
    node_count = lax.axis_size("node")
    slot_count = fetch_pick.shape[1]
    stride = node_count // slot_count
    part, width = tokens.shape
    order = ring_order(lax.axis_size("local"))
    size = len(order)

    picked = pick_pass(list(range(slot_count)), node_count, fetch_pick, panels)
    read = [from_behind(picked[r], "node", r * stride) if r else picked[r] for r in range(slot_count)]

    x_parts = ring_gather(tokens, order, size // 2)
    dy_parts = ring_gather(cotangent, order, size - 1 - size // 2)

    ring_routes = routes.reshape(size, part)
    ring_weight = route_weight.reshape(size, part)

    near = [d for d in range(size) if min(d, size - d) <= size // 4 and d != size // 4]
    groups = [near, [d for d in range(size) if d not in near]]

    def make_acts(r, g, after=()):
        take = groups[g]
        return acts_pass(
            "nf"[g],
            r,
            take,
            [x_parts[d] for d in take],
            [dy_parts[d] for d in take],
            read[r],
            ring_routes,
            ring_weight,
            after,
        )

    rows = [d for group in groups for d in group]

    def make_grads(r, after=()):
        return grads_pass(
            r,
            [x_parts[d] for d in rows],
            [dy_parts[d] for d in rows],
            acts[r],
            read[r].shape,
            after,
        )

    acts, grads = [None] * slot_count, [None] * slot_count
    last = slot_count // 2
    turn = [r for r in range(1, slot_count) if r != last] + [0]
    acts_near = {r: make_acts(r, 0) for r in turn}
    done = ()
    for r in turn:
        acts[r] = (acts_near[r], make_acts(r, 1, done))
        done = (acts[r][1],)
        if r == turn[0]:
            grads[r] = make_grads(r)
            done = (grads[r],)
    acts[last] = (make_acts(last, 0, done), make_acts(last, 1))

    first = size // 2
    early = [("mixed", first), ("grad", size - 1 - first), ("mixed", first + 1), ("grad", first)]
    late = [
        (kind, d)
        for hop in range(first, -1, -1)
        for d in {hop: 0, size - hop: 0}
        if d < size
        for kind in ("mixed", "grad")
        if (kind, d) not in early
    ]
    chunks = dict(zip(early, chunk_pass(early, acts, read, groups, part)))
    done = (chunks[early[0]],)
    for r in turn[1:-1] + [last]:
        grads[r] = make_grads(r, done)
        done = (grads[r],)
    chunks.update(zip(late, chunk_pass(late, acts, read, groups, part, done)))
    grads[0] = make_grads(0, (chunks[late[0]],))
    mixed = ring_scatter([chunks["mixed", d] for d in range(size)], order, size // 2)
    token_grad = ring_scatter([chunks["grad", d] for d in range(size)], order, size - 1 - size // 2)

    grads = [
        from_behind(grads[r], "node", node_count - r * stride) if r else grads[r]
        for r in range(slot_count)
    ]
    panel_grad = total_pass(node_count, fetch_pick, grads, panels.shape)
    return mixed, token_grad, panel_grad


def solution(mesh):
    return jax.shard_map(
        body,
        mesh=mesh,
        in_specs=(
            P(("node", "local"), None),
            P(("node", "local"), None),
            P("node", None),
            P("node", None),
            P(),
            P("node", None, "local", None),
        ),
        out_specs=(
            P(("node", "local"), None),
            P(("node", "local"), None),
            P("node", None, "local", None),
        ),
        check_vma=False,
    )
```

```python
import jax
import jax.numpy as jnp
from jax import lax
from jax.experimental import pallas as pl
from jax.experimental.pallas import tpu as pltpu
from jax.sharding import PartitionSpec as P

BF16 = jnp.bfloat16
F32 = jnp.float32
VMEM_LIMIT = 24 * 1024 * 1024
NO_COST = pl.CostEstimate(flops=1, bytes_accessed=1, transcendentals=0)


def work_cost(flops):
    return pl.CostEstimate(flops=flops, bytes_accessed=1, transcendentals=0)


CONTRACT_LAST = (((1,), (1,)), ((), ()))
CONTRACT_FIRST = (((0,), (0,)), ((), ()))


def whole_in_vmem():
    return pl.BlockSpec(memory_space=pltpu.VMEM)


def untouched():
    return pl.BlockSpec(memory_space=pl.ANY)


def tile_of(size, most):
    tile = min(size, most)
    while size % tile:
        tile -= 1
    return tile


def ring_order(size):
    return list(range(0, size, 2)) + list(range(1, size, 2))[::-1]


def ring_source(size, ahead):
    me = lax.axis_index("local")
    half = lax.div(size + 1, 2)
    place = jnp.where(lax.rem(me, 2) == 0, lax.div(me, 2), size - 1 - lax.div(me, 2))
    there = lax.rem(place + ahead, size)
    return jnp.where(there < half, 2 * there, 2 * (size - 1 - there) + 1)


def partner_of(place, turn, slots):
    return place ^ turn


def owner_of(node, turn, slots, stride):
    return partner_of(node // stride, turn, slots) * stride + node % stride


def turn_slot(turn, slots, stride):
    place = lax.div(lax.axis_index("node"), stride)
    return lax.rem(place - partner_of(place, turn, slots) + slots, slots)


def turn_pick(fetch_pick, turn, stride):
    slots = fetch_pick.shape[1]
    node = lax.axis_index("node")
    place = lax.div(node, stride)
    partner = partner_of(place, turn, slots)
    reader = partner * stride + lax.rem(node, stride)
    return fetch_pick[reader, lax.rem(partner - place + slots, slots)]


def exchange(block, turn, slots):
    size = lax.axis_size("node")
    stride = size // slots
    return lax.ppermute(
        block, "node", [(owner_of(node, turn, slots, stride), node) for node in range(size)]
    )


def pick_kernel(turns, stride, fetch_pick, panels, *refs):
    out, sems = refs[-2:]
    copies = [
        pltpu.make_async_copy(panels.at[turn_pick(fetch_pick, turn, stride)], out.at[i], sems.at[i])
        for i, turn in enumerate(turns)
    ]
    for copy in copies:
        copy.start()
    for copy in copies:
        copy.wait()


def pick_pass(turns, stride, fetch_pick, panels, after=()):
    return pl.pallas_call(
        lambda *refs: pick_kernel(turns, stride, *refs),
        out_shape=jax.ShapeDtypeStruct((len(turns),) + panels.shape[1:], BF16),
        in_specs=[pl.BlockSpec(memory_space=pltpu.SMEM), untouched()] + [untouched()] * len(after),
        out_specs=untouched(),
        scratch_shapes=[pltpu.SemaphoreType.DMA((len(turns),))],
        compiler_params=pltpu.CompilerParams(vmem_limit_bytes=1024 * 1024),
        name="pick",
    )(fetch_pick, panels, *after)


def gate(value, after):
    return pl.pallas_call(
        lambda *refs: None,
        out_shape=jax.ShapeDtypeStruct(value.shape, value.dtype),
        in_specs=[untouched()] * (1 + len(after)),
        out_specs=untouched(),
        input_output_aliases={0: 0},
        compiler_params=pltpu.CompilerParams(vmem_limit_bytes=1024 * 1024),
        cost_estimate=NO_COST,
        name="gate",
    )(value, *after)


def total_kernel(turns, stride, counts, fetch_pick, *refs):
    out, refs = refs[-1], list(refs[: sum(counts)])
    picks = [turn_pick(fetch_pick, turn, stride) for turn in turns]
    experts, kinds = out.shape[:2]
    grads = []
    for count in counts:
        taken, refs = refs[:count], refs[count:]
        grads.append([taken[0].at[kind] for kind in range(kinds)] if count == 1 else taken)
    for kind in range(kinds):
        terms = [grad[kind][...].astype(F32) for grad in grads]
        for e in range(experts):
            total = jnp.zeros(terms[0].shape, F32)
            for pick, term in zip(picks, terms):
                total += jnp.where(pick == e, term, 0.0)
            out[e, kind] = total.astype(BF16)


def total_pass(turns, stride, fetch_pick, grads, shape, after):
    counts = [len(grad) for grad in grads]
    return pl.pallas_call(
        lambda *refs: total_kernel(turns, stride, counts, *refs),
        out_shape=jax.ShapeDtypeStruct(shape, BF16),
        in_specs=[pl.BlockSpec(memory_space=pltpu.SMEM)]
        + [whole_in_vmem()] * sum(counts)
        + [untouched()] * len(after),
        out_specs=whole_in_vmem(),
        compiler_params=pltpu.CompilerParams(vmem_limit_bytes=VMEM_LIMIT),
        cost_estimate=NO_COST,
        name="total",
    )(fetch_pick, *[grad for slot_grads in grads for grad in slot_grads], *after)


def add_kernel(turn, stride, fetch_pick, total, grad, out, sums, terms, in_sems, out_sems):
    pick = turn_pick(fetch_pick, turn, stride)
    kinds = grad.shape[0]
    reads = [
        (
            pltpu.make_async_copy(total.at[pick, kind], sums.at[kind], in_sems.at[kind]),
            pltpu.make_async_copy(grad.at[kind], terms.at[kind], in_sems.at[kinds + kind]),
        )
        for kind in range(kinds)
    ]
    writes = [
        pltpu.make_async_copy(sums.at[kind], out.at[pick, kind], out_sems.at[kind])
        for kind in range(kinds)
    ]
    for first, second in reads:
        first.start()
        second.start()
    for kind in range(kinds):
        for read in reads[kind]:
            read.wait()
        sums[kind] = (sums[kind].astype(F32) + terms[kind].astype(F32)).astype(BF16)
        writes[kind].start()
    for write in writes:
        write.wait()


def add_pass(turn, stride, fetch_pick, total, grad):
    kinds = grad.shape[0]
    return pl.pallas_call(
        lambda *refs: add_kernel(turn, stride, *refs),
        out_shape=jax.ShapeDtypeStruct(total.shape, BF16),
        in_specs=[pl.BlockSpec(memory_space=pltpu.SMEM), untouched(), untouched()],
        out_specs=untouched(),
        input_output_aliases={1: 0},
        scratch_shapes=[
            pltpu.VMEM(grad.shape, BF16),
            pltpu.VMEM(grad.shape, BF16),
            pltpu.SemaphoreType.DMA((2 * kinds,)),
            pltpu.SemaphoreType.DMA((kinds,)),
        ],
        compiler_params=pltpu.CompilerParams(vmem_limit_bytes=8 * 1024 * 1024),
        name="add",
    )(fetch_pick, total, grad)


def ring_step(block, order, distance):
    size = len(order)
    return lax.ppermute(
        block, "local", [(order[i], order[(i + distance) % size]) for i in range(size)]
    )


def add_rows_kernel(*refs):
    a, b, out = refs[0], refs[1], refs[-1]
    out[...] = (a[...].astype(F32) + b[...].astype(F32)).astype(out.dtype)


def add_rows(a, b, dtype, after=()):
    return pl.pallas_call(
        add_rows_kernel,
        out_shape=jax.ShapeDtypeStruct(a.shape, dtype),
        in_specs=[whole_in_vmem()] * 2 + [untouched()] * len(after),
        out_specs=whole_in_vmem(),
        compiler_params=pltpu.CompilerParams(vmem_limit_bytes=VMEM_LIMIT),
        cost_estimate=NO_COST,
        name="add_rows",
    )(a, b, *after)


def acts_kernel(turn, slots, stride, size, offsets, *refs):
    parts = len(offsets)
    x_refs, dy_refs = refs[:parts], refs[parts : 2 * parts]
    panel, routes, weight, acts = *refs[2 * parts : 2 * parts + 3], refs[-1]
    units, width = panel.shape[1:]
    part = x_refs[0].shape[0]
    at_once = 2 if parts % 2 == 0 else 1
    slot = turn_slot(turn, slots, stride)
    for d in range(0, parts, at_once):
        here = slice(d * part, (d + at_once) * part)
        x = jnp.concatenate([ref[...] for ref in x_refs[d : d + at_once]], axis=0)
        dy = jnp.concatenate([ref[...] for ref in dy_refs[d : d + at_once]], axis=0)
        both = lax.dot_general(
            panel[0:2].reshape(2 * units, width), x, CONTRACT_LAST, preferred_element_type=F32
        )
        gate, up = both[:units], both[units:]
        d_hidden = lax.dot_general(panel[2], dy, CONTRACT_LAST, preferred_element_type=F32)
        sources = [ring_source(size, ahead) for ahead in offsets[d : d + at_once]]
        scale = jnp.concatenate(
            [
                jnp.where(routes[pl.ds(i, 1), :] == slot, weight[pl.ds(i, 1), :], 0.0)
                for i in sources
            ],
            axis=1,
        )
        sigmoid_gate = jax.nn.sigmoid(gate)
        activated = gate * sigmoid_gate
        d_hidden = d_hidden * scale
        d_gate = d_hidden * up * sigmoid_gate * (1.0 + gate * (1.0 - sigmoid_gate))
        acts[0:units, here] = d_gate.astype(BF16)
        acts[units : 2 * units, here] = (d_hidden * activated).astype(BF16)
        acts[2 * units : 3 * units, here] = (activated * up * scale).astype(BF16)


def acts_pass(name, turn, slots, stride, offsets, x_parts, dy_parts, panel, routes, weight, after=()):
    parts = len(x_parts)
    part = x_parts[0].shape[0]
    return pl.pallas_call(
        lambda *refs: acts_kernel(turn, slots, stride, routes.shape[0], offsets, *refs),
        out_shape=jax.ShapeDtypeStruct((3 * panel.shape[1], parts * part), BF16),
        in_specs=[whole_in_vmem()] * (2 * parts + 3) + [untouched()] * len(after),
        out_specs=whole_in_vmem(),
        compiler_params=pltpu.CompilerParams(vmem_limit_bytes=VMEM_LIMIT),
        cost_estimate=work_cost(6 * parts * part * panel.shape[1] * panel.shape[2]),
        name=f"acts_{turn}_{name}",
    )(*x_parts, *dy_parts, panel, routes, weight, *after)


def grads_kernel(parts, groups, kinds, *refs):
    x_refs, dy_refs = refs[:parts], refs[parts : 2 * parts]
    acts, grads = refs[2 * parts : 2 * parts + groups], refs[-kinds:]
    if kinds == 1:
        grads = [grads[0].at[kind] for kind in range(3)]
    units, width = grads[0].shape
    columns = tile_of(width, 512)
    for start in range(0, width, columns):
        here = slice(start, start + columns)
        x = jnp.concatenate([ref[:, here] for ref in x_refs], axis=0)
        dy = jnp.concatenate([ref[:, here] for ref in dy_refs], axis=0)
        d_both = jnp.concatenate([act[0 : 2 * units, :] for act in acts], axis=1)
        d_both = jnp.dot(d_both, x, preferred_element_type=F32).astype(BF16)
        grads[0][:, here] = d_both[0:units]
        grads[1][:, here] = d_both[units:]
        hidden = jnp.concatenate([act[2 * units : 3 * units, :] for act in acts], axis=1)
        grads[2][:, here] = jnp.dot(hidden, dy, preferred_element_type=F32).astype(BF16)


def grads_pass(turn, x_parts, dy_parts, acts, shapes, after=()):
    parts = len(x_parts)
    return pl.pallas_call(
        lambda *refs: grads_kernel(parts, len(acts), len(shapes), *refs),
        out_shape=tuple(jax.ShapeDtypeStruct(shape, BF16) for shape in shapes),
        in_specs=[whole_in_vmem()] * (2 * parts + len(acts)) + [untouched()] * len(after),
        out_specs=tuple(whole_in_vmem() for _ in shapes),
        compiler_params=pltpu.CompilerParams(vmem_limit_bytes=VMEM_LIMIT),
        cost_estimate=work_cost(6 * parts * acts[0].shape[0] // 3 * x_parts[0].size),
        name=f"grads_{turn}",
    )(*x_parts, *dy_parts, *acts, *after)


def chunk_kernel(wanted, slots, part, acts, panels, outs):
    units, width = panels[0].shape[1:]
    columns = tile_of(width, 512)

    @pl.loop(0, width // columns)
    def _(step):
        here = pl.ds(pl.multiple_of(step * columns, columns), columns)
        kinds = {"mixed": (2, 3), "grad": (0, 2)}
        sides = {
            kind: jnp.concatenate(
                [panel[which, :, here] for panel in panels for which in range(*span)], axis=0
            )
            for kind, span in kinds.items()
        }
        for out, (kind, group, row) in zip(outs, wanted):
            low, high = (units * which for which in kinds[kind])
            act = jnp.concatenate(
                [act[group][low:high, row * part : (row + 1) * part] for act in acts], axis=0
            )
            total = lax.dot_general(act, sides[kind], CONTRACT_FIRST, preferred_element_type=F32)
            out[:, here] = total.astype(BF16)


def chunk_pass(wanted, acts, panels, groups, part, after=()):
    slots = len(panels)
    width = panels[0].shape[2]
    named = [
        (kind, g, group.index(d)) for kind, d in wanted for g, group in enumerate(groups) if d in group
    ]

    def kernel(*refs):
        act_refs = [refs[s * len(groups) : (s + 1) * len(groups)] for s in range(slots)]
        rest = refs[slots * len(groups) :]
        chunk_kernel(named, slots, part, act_refs, rest[:slots], rest[slots + len(after) :])

    return pl.pallas_call(
        kernel,
        out_shape=tuple(jax.ShapeDtypeStruct((part, width), BF16) for _ in wanted),
        in_specs=[whole_in_vmem()] * (slots * len(groups) + slots) + [untouched()] * len(after),
        out_specs=tuple(whole_in_vmem() for _ in wanted),
        compiler_params=pltpu.CompilerParams(vmem_limit_bytes=VMEM_LIMIT),
        cost_estimate=NO_COST,
        name=f"chunks_{len(wanted)}",
    )(*[act for slot_acts in acts for act in slot_acts], *panels, *after)


class Line:
    def __init__(self):
        self.tail = ()

    def step(self, make):
        out = make(self.tail)
        self.tail = (out[0] if isinstance(out, (tuple, list)) else out,)
        return out

    def arrive(self, value):
        return self.step(lambda after: gate(value, after))


def body(tokens, cotangent, routes, route_weight, fetch_pick, panels):
    slots = fetch_pick.shape[1]
    stride = lax.axis_size("node") // slots
    part, width = tokens.shape
    order = ring_order(lax.axis_size("local"))
    size = len(order)
    up_most, down_most = size // 2, size - 1 - size // 2
    last, late = slots - 1, slots - 2
    middle = list(range(1, late))
    line = Line()

    ring_routes = routes.reshape(size, part)
    ring_weight = route_weight.reshape(size, part)
    near = [d for d in range(size) if min(d, size - d) <= size // 4 and d != size // 4]
    groups = [near, [d for d in range(size) if d not in near]]
    rows = [d for group in groups for d in group]
    x_parts = [tokens] + [None] * (size - 1)
    dy_parts = [cotangent] + [None] * (size - 1)
    acts = [[None, None] for _ in range(slots)]
    grads, back = [None] * slots, [None] * slots

    def pick(turn):
        return line.step(lambda after: pick_pass([turn], stride, fetch_pick, panels, after))[0]

    def make_acts(turn, g):
        take = groups[g]
        acts[turn][g] = line.step(
            lambda after: acts_pass(
                "nf"[g],
                turn,
                slots,
                stride,
                take,
                [x_parts[d] for d in take],
                [dy_parts[d] for d in take],
                read[turn],
                ring_routes,
                ring_weight,
                after,
            )
        )

    def make_grads(turn):
        shape = read[turn].shape
        grads[turn] = line.step(
            lambda after: grads_pass(
                turn,
                [x_parts[d] for d in rows],
                [dy_parts[d] for d in rows],
                acts[turn],
                [shape[1:]] * shape[0] if turn in middle else [shape],
                after,
            )
        )
        if turn != last:
            back[turn] = [exchange(grad, turn, slots) if turn else grad for grad in grads[turn]]

    read = [None] * slots
    read[late] = exchange(pick(late), late, slots)
    for turn in middle:
        read[turn] = exchange(pick(turn), turn, slots)
    read[last], read[0] = pick(last), pick(0)

    chains = [(x_parts, 1, up_most), (dy_parts, -1, up_most), (x_parts, -1, down_most), (dy_parts, 1, down_most)]
    moving = [ring_step(parts[0], order, way) for parts, way, _ in chains]
    for turn in middle:
        read[turn] = line.arrive(read[turn])
    for hop in range(1, up_most + 1):
        for i, (parts, way, hops) in enumerate(chains):
            if hop > hops:
                continue
            if hop == max(1, up_most // 2) and i == 2:
                read[late] = line.arrive(read[late])
                read[last] = exchange(line.arrive(read[last]), last, slots)
            arrived = line.arrive(moving[i])
            parts[-way * hop % size] = arrived
            if hop < hops:
                moving[i] = ring_step(arrived, order, way)
            if hop == max(1, up_most // 2) and i == len(chains) - 1:
                for turn in middle + [0]:
                    make_acts(turn, 0)

    for turn in middle:
        make_acts(turn, 1)
        make_grads(turn)
    make_acts(late, 0)
    make_acts(late, 1)
    make_grads(late)
    make_acts(0, 1)
    for turn in middle:
        back[turn] = [line.arrive(grad) for grad in back[turn]]
    read[last] = line.arrive(read[last])
    make_acts(last, 1)
    make_acts(last, 0)

    kinds = ("mixed", "grad")
    early = [("mixed", up_most), ("grad", size - up_most), ("mixed", size - down_most), ("grad", down_most)]
    later = [(kind, d) for kind in kinds for d in range(size) if (kind, d) not in early]
    chunks = dict(zip(early, line.step(lambda after: chunk_pass(early, acts, read, groups, part, after))))
    chains = [("mixed", 1, up_most), ("grad", -1, up_most), ("mixed", -1, down_most), ("grad", 1, down_most)]
    moving = [ring_step(chunks[kind, way * hops % size], order, way) for kind, way, hops in chains]
    chunks.update(zip(later, line.step(lambda after: chunk_pass(later, acts, read, groups, part, after))))
    make_grads(last)
    make_grads(0)

    sums = {}
    for hop in range(1, up_most + 1):
        for i, (kind, way, hops) in enumerate(chains):
            if hop > hops:
                continue
            if hop == max(1, up_most // 2) and i == 2:
                back[late] = [line.arrive(back[late][0])]
                back[last] = exchange(line.arrive(grads[last][0]), last, slots)
            left = hops - hop
            if left:
                chunk = chunks[kind, way * left % size]
                arrived = line.step(lambda after: add_rows(moving[i], chunk, BF16, after))
                moving[i] = ring_step(arrived, order, way)
                if left == 1 and i == 1:
                    near_total = line.step(
                        lambda after: total_pass(
                            list(range(last)), stride, fetch_pick, back[:last], panels.shape, after
                        )
                    )
            elif kind not in sums:
                sums[kind] = line.step(lambda after: add_rows(moving[i], chunks[kind, 0], F32, after))
            else:
                sums[kind] = line.step(lambda after: add_rows(moving[i], sums[kind], BF16, after))
    panel_grad = add_pass(last, stride, fetch_pick, near_total, back[last])
    return sums["mixed"], sums["grad"], panel_grad


def solution(mesh):
    return jax.shard_map(
        body,
        mesh=mesh,
        in_specs=(
            P(("node", "local"), None),
            P(("node", "local"), None),
            P("node", None),
            P("node", None),
            P(),
            P("node", None, "local", None),
        ),
        out_specs=(
            P(("node", "local"), None),
            P(("node", "local"), None),
            P("node", None, "local", None),
        ),
        check_vma=False,
    )
```

```python
import jax
import jax.numpy as jnp
from jax import lax
from jax.experimental import pallas as pl
from jax.experimental.pallas import tpu as pltpu
from jax.sharding import PartitionSpec as P

BF16 = jnp.bfloat16
F32 = jnp.float32
VMEM_LIMIT = 24 * 1024 * 1024
NO_COST = pl.CostEstimate(flops=1, bytes_accessed=1, transcendentals=0)


LAST_FLOPS = 12 * 10**9


def work_cost(flops):
    return pl.CostEstimate(flops=flops, bytes_accessed=1, transcendentals=0)


CONTRACT_LAST = (((1,), (1,)), ((), ()))
CONTRACT_FIRST = (((0,), (0,)), ((), ()))


def whole_in_vmem():
    return pl.BlockSpec(memory_space=pltpu.VMEM)


def in_hbm():
    return pl.BlockSpec(memory_space=pltpu.HBM)


def token_shape():
    return jax.ShapeDtypeStruct((8, 128), F32)


def untouched():
    return pl.BlockSpec(memory_space=pl.ANY)


def tile_of(size, most):
    tile = min(size, most)
    while size % tile:
        tile -= 1
    return tile


def ring_order(size):
    return list(range(0, size, 2)) + list(range(1, size, 2))[::-1]


def ring_source(size, ahead):
    me = lax.axis_index("local")
    half = lax.div(size + 1, 2)
    place = jnp.where(lax.rem(me, 2) == 0, lax.div(me, 2), size - 1 - lax.div(me, 2))
    there = lax.rem(place + ahead, size)
    return jnp.where(there < half, 2 * there, 2 * (size - 1 - there) + 1)


def partner_of(place, turn, slots):
    return place ^ turn


def owner_of(node, turn, slots, stride):
    return partner_of(node // stride, turn, slots) * stride + node % stride


def turn_slot(turn, slots, stride):
    place = lax.div(lax.axis_index("node"), stride)
    return lax.rem(place - partner_of(place, turn, slots) + slots, slots)


def turn_pick(fetch_pick, turn, stride):
    slots = fetch_pick.shape[1]
    node = lax.axis_index("node")
    place = lax.div(node, stride)
    partner = partner_of(place, turn, slots)
    reader = partner * stride + lax.rem(node, stride)
    return fetch_pick[reader, lax.rem(partner - place + slots, slots)]


def exchange(block, turn, slots):
    size = lax.axis_size("node")
    stride = size // slots
    return lax.ppermute(
        block, "node", [(owner_of(node, turn, slots, stride), node) for node in range(size)]
    )


def pick_kernel(turns, stride, fetch_pick, panels, *refs):
    outs, sems = refs[-len(turns) - 1 : -1], refs[-1]
    copies = [
        pltpu.make_async_copy(panels.at[turn_pick(fetch_pick, turn, stride)], out, sems.at[i])
        for i, (turn, out) in enumerate(zip(turns, outs))
    ]
    for copy in copies:
        copy.start()
    for copy in copies:
        copy.wait()


def pick_pass(turns, stride, fetch_pick, panels, after=()):
    return pl.pallas_call(
        lambda *refs: pick_kernel(turns, stride, *refs),
        out_shape=tuple(jax.ShapeDtypeStruct(panels.shape[1:], BF16) for _ in turns),
        in_specs=[pl.BlockSpec(memory_space=pltpu.SMEM), in_hbm()] + [untouched()] * len(after),
        out_specs=tuple(untouched() for _ in turns),
        scratch_shapes=[pltpu.SemaphoreType.DMA((len(turns),))],
        compiler_params=pltpu.CompilerParams(vmem_limit_bytes=1024 * 1024),
        cost_estimate=NO_COST,
        name="pick",
    )(fetch_pick, panels, *after)


def gate(value, after):
    return pl.pallas_call(
        lambda *refs: None,
        out_shape=jax.ShapeDtypeStruct(value.shape, value.dtype),
        in_specs=[untouched()] * (1 + len(after)),
        out_specs=untouched(),
        input_output_aliases={0: 0},
        compiler_params=pltpu.CompilerParams(vmem_limit_bytes=1024 * 1024),
        cost_estimate=NO_COST,
        name="gate",
    )(value, *after)


def total_kernel(turns, last, stride, counts, fetch_pick, *refs):
    out, base, token, refs = *refs[-3:], list(refs[: sum(counts)])
    picks = [turn_pick(fetch_pick, turn, stride) for turn in turns]
    last_pick = turn_pick(fetch_pick, last, stride)
    token[...] = jnp.zeros_like(token)
    experts, kinds = out.shape[:2]
    grads = []
    for count in counts:
        taken, refs = refs[:count], refs[count:]
        grads.append([taken[0].at[kind] for kind in range(kinds)] if count == 1 else taken)
    for kind in range(kinds):
        terms = [grad[kind][...].astype(F32) for grad in grads]
        for e in range(experts):
            total = jnp.zeros(terms[0].shape, F32)
            for pick, term in zip(picks, terms):
                total += jnp.where(pick == e, term, 0.0)
            total = total.astype(BF16)
            out[e, kind] = total
            if e == 0:
                base[kind] = total
            else:

                @pl.when(last_pick == e)
                def _():
                    base[kind] = total


def total_pass(turns, last, stride, fetch_pick, grads, shape, after):
    counts = [len(grad) for grad in grads]
    return pl.pallas_call(
        lambda *refs: total_kernel(turns, last, stride, counts, *refs),
        out_shape=(
            jax.ShapeDtypeStruct(shape, BF16),
            jax.ShapeDtypeStruct(shape[1:], BF16),
            token_shape(),
        ),
        in_specs=[pl.BlockSpec(memory_space=pltpu.SMEM)]
        + [whole_in_vmem()] * sum(counts)
        + [untouched()] * len(after),
        out_specs=(whole_in_vmem(),) * 3,
        compiler_params=pltpu.CompilerParams(vmem_limit_bytes=VMEM_LIMIT),
        cost_estimate=NO_COST,
        name="total",
    )(fetch_pick, *[grad for slot_grads in grads for grad in slot_grads], *after)


def add_kernel(turn, stride, fetch_pick, total, base, grad, out, sums, sems):
    pick = turn_pick(fetch_pick, turn, stride)
    writes = [
        pltpu.make_async_copy(sums.at[kind], out.at[pick, kind], sems.at[kind])
        for kind in range(grad.shape[0])
    ]
    for kind, write in enumerate(writes):
        sums[kind] = (base[kind].astype(F32) + grad[kind].astype(F32)).astype(BF16)
        write.start()
    for write in writes:
        write.wait()


def add_pass(turn, stride, fetch_pick, total, base, grad):
    return pl.pallas_call(
        lambda *refs: add_kernel(turn, stride, *refs),
        out_shape=jax.ShapeDtypeStruct(total.shape, BF16),
        in_specs=[pl.BlockSpec(memory_space=pltpu.SMEM), in_hbm(), whole_in_vmem(), whole_in_vmem()],
        out_specs=in_hbm(),
        input_output_aliases={1: 0},
        scratch_shapes=[pltpu.VMEM(grad.shape, BF16), pltpu.SemaphoreType.DMA((grad.shape[0],))],
        compiler_params=pltpu.CompilerParams(vmem_limit_bytes=12 * 1024 * 1024),
        cost_estimate=NO_COST,
        name="add",
    )(fetch_pick, total, base, grad)


def ring_step(block, order, distance):
    size = len(order)
    return lax.ppermute(
        block, "local", [(order[i], order[(i + distance) % size]) for i in range(size)]
    )


def add_rows_kernel(*refs):
    a, b, out = refs[0], refs[1], refs[-1]
    out[...] = (a[...].astype(F32) + b[...].astype(F32)).astype(out.dtype)


def add_rows(a, b, dtype, after=()):
    return pl.pallas_call(
        add_rows_kernel,
        out_shape=jax.ShapeDtypeStruct(a.shape, dtype),
        in_specs=[whole_in_vmem()] * 2 + [untouched()] * len(after),
        out_specs=whole_in_vmem(),
        compiler_params=pltpu.CompilerParams(vmem_limit_bytes=VMEM_LIMIT),
        cost_estimate=NO_COST,
        name="add_rows",
    )(a, b, *after)


def acts_kernel(turn, slots, stride, size, offsets, *refs):
    parts = len(offsets)
    x_refs, dy_refs = refs[:parts], refs[parts : 2 * parts]
    panel, routes, weight, acts = *refs[2 * parts : 2 * parts + 3], refs[-1]
    units, width = panel.shape[1:]
    part = x_refs[0].shape[0]
    at_once = 2 if parts % 2 == 0 else 1
    slot = turn_slot(turn, slots, stride)
    for d in range(0, parts, at_once):
        here = slice(d * part, (d + at_once) * part)
        x = jnp.concatenate([ref[...] for ref in x_refs[d : d + at_once]], axis=0)
        dy = jnp.concatenate([ref[...] for ref in dy_refs[d : d + at_once]], axis=0)
        both = lax.dot_general(
            panel[0:2].reshape(2 * units, width), x, CONTRACT_LAST, preferred_element_type=F32
        )
        gate, up = both[:units], both[units:]
        d_hidden = lax.dot_general(panel[2], dy, CONTRACT_LAST, preferred_element_type=F32)
        sources = [ring_source(size, ahead) for ahead in offsets[d : d + at_once]]
        scale = jnp.concatenate(
            [
                jnp.where(routes[pl.ds(i, 1), :] == slot, weight[pl.ds(i, 1), :], 0.0)
                for i in sources
            ],
            axis=1,
        )
        sigmoid_gate = jax.nn.sigmoid(gate)
        activated = gate * sigmoid_gate
        d_hidden = d_hidden * scale
        d_gate = d_hidden * up * sigmoid_gate * (1.0 + gate * (1.0 - sigmoid_gate))
        acts[0:units, here] = d_gate.astype(BF16)
        acts[units : 2 * units, here] = (d_hidden * activated).astype(BF16)
        acts[2 * units : 3 * units, here] = (activated * up * scale).astype(BF16)


def acts_pass(name, turn, slots, stride, offsets, x_parts, dy_parts, panel, routes, weight, after=()):
    parts = len(x_parts)
    part = x_parts[0].shape[0]
    return pl.pallas_call(
        lambda *refs: acts_kernel(turn, slots, stride, routes.shape[0], offsets, *refs),
        out_shape=jax.ShapeDtypeStruct((3 * panel.shape[1], parts * part), BF16),
        in_specs=[whole_in_vmem()] * (2 * parts + 3) + [untouched()] * len(after),
        out_specs=whole_in_vmem(),
        compiler_params=pltpu.CompilerParams(vmem_limit_bytes=VMEM_LIMIT),
        cost_estimate=work_cost(6 * parts * part * panel.shape[1] * panel.shape[2]),
        name=f"acts_{turn}_{name}",
    )(*x_parts, *dy_parts, panel, routes, weight, *after)


def grads_kernel(parts, groups, kinds, *refs):
    x_refs, dy_refs = refs[:parts], refs[parts : 2 * parts]
    acts, grads = refs[2 * parts : 2 * parts + groups], refs[-kinds:]
    if kinds == 1:
        grads = [grads[0].at[kind] for kind in range(3)]
    units, width = grads[0].shape
    columns = tile_of(width, 512)
    for start in range(0, width, columns):
        here = slice(start, start + columns)
        x = jnp.concatenate([ref[:, here] for ref in x_refs], axis=0)
        dy = jnp.concatenate([ref[:, here] for ref in dy_refs], axis=0)
        d_both = jnp.concatenate([act[0 : 2 * units, :] for act in acts], axis=1)
        d_both = jnp.dot(d_both, x, preferred_element_type=F32).astype(BF16)
        grads[0][:, here] = d_both[0:units]
        grads[1][:, here] = d_both[units:]
        hidden = jnp.concatenate([act[2 * units : 3 * units, :] for act in acts], axis=1)
        grads[2][:, here] = jnp.dot(hidden, dy, preferred_element_type=F32).astype(BF16)


def grads_pass(turn, x_parts, dy_parts, acts, shapes, after=()):
    parts = len(x_parts)
    return pl.pallas_call(
        lambda *refs: grads_kernel(parts, len(acts), len(shapes), *refs),
        out_shape=tuple(jax.ShapeDtypeStruct(shape, BF16) for shape in shapes),
        in_specs=[whole_in_vmem()] * (2 * parts + len(acts)) + [untouched()] * len(after),
        out_specs=tuple(whole_in_vmem() for _ in shapes),
        compiler_params=pltpu.CompilerParams(vmem_limit_bytes=VMEM_LIMIT),
        cost_estimate=work_cost(6 * parts * acts[0].shape[0] // 3 * x_parts[0].size),
        name=f"grads_{turn}",
    )(*x_parts, *dy_parts, *acts, *after)


def chunk_kernel(wanted, slots, part, acts, panels, outs):
    units, width = panels[0].shape[1:]
    columns = tile_of(width, 512)

    @pl.loop(0, width // columns)
    def _(step):
        here = pl.ds(pl.multiple_of(step * columns, columns), columns)
        kinds = {"mixed": (2, 3), "grad": (0, 2)}
        sides = {
            kind: jnp.concatenate(
                [panel[which, :, here] for panel in panels for which in range(*span)], axis=0
            )
            for kind, span in kinds.items()
        }
        for out, (kind, group, row) in zip(outs, wanted):
            low, high = (units * which for which in kinds[kind])
            act = jnp.concatenate(
                [act[group][low:high, row * part : (row + 1) * part] for act in acts], axis=0
            )
            total = lax.dot_general(act, sides[kind], CONTRACT_FIRST, preferred_element_type=F32)
            out[:, here] = total.astype(BF16)


def chunk_pass(wanted, acts, panels, groups, part, cost, after=()):
    slots = len(panels)
    width = panels[0].shape[2]
    named = [
        (kind, g, group.index(d)) for kind, d in wanted for g, group in enumerate(groups) if d in group
    ]

    def kernel(*refs):
        act_refs = [refs[s * len(groups) : (s + 1) * len(groups)] for s in range(slots)]
        rest = refs[slots * len(groups) :]
        chunk_kernel(named, slots, part, act_refs, rest[:slots], rest[slots + len(after) :])

    return pl.pallas_call(
        kernel,
        out_shape=tuple(jax.ShapeDtypeStruct((part, width), BF16) for _ in wanted),
        in_specs=[whole_in_vmem()] * (slots * len(groups) + slots) + [untouched()] * len(after),
        out_specs=tuple(whole_in_vmem() for _ in wanted),
        compiler_params=pltpu.CompilerParams(vmem_limit_bytes=VMEM_LIMIT),
        cost_estimate=cost,
        name=f"chunks_{len(wanted)}",
    )(*[act for slot_acts in acts for act in slot_acts], *panels, *after)


def final_rows_kernel(*refs):
    a, b, out, token = refs[0], refs[1], *refs[-2:]
    out[...] = (a[...].astype(F32) + b[...]).astype(out.dtype)
    token[...] = jnp.zeros_like(token)


def final_rows(a, b, cost, after):
    return pl.pallas_call(
        final_rows_kernel,
        out_shape=(jax.ShapeDtypeStruct(a.shape, BF16), token_shape()),
        in_specs=[whole_in_vmem()] * 2 + [untouched()] * len(after),
        out_specs=(whole_in_vmem(), whole_in_vmem()),
        compiler_params=pltpu.CompilerParams(vmem_limit_bytes=VMEM_LIMIT),
        cost_estimate=cost,
        name="final_rows",
    )(a, b, *after)


class Line:
    def __init__(self):
        self.tail = ()

    def step(self, make):
        out = make(self.tail)
        self.tail = (out[-1] if isinstance(out, (tuple, list)) else out,)
        return out

    def arrive(self, value):
        return self.step(lambda after: gate(value, after))


def body(tokens, cotangent, routes, route_weight, fetch_pick, panels):
    slots = fetch_pick.shape[1]
    stride = lax.axis_size("node") // slots
    part, width = tokens.shape
    order = ring_order(lax.axis_size("local"))
    size = len(order)
    up_most, down_most = size // 2, size - 1 - size // 2
    last, late = slots - 1, slots - 2
    middle = list(range(1, late))
    line = Line()

    ring_routes = routes.reshape(size, part)
    ring_weight = route_weight.reshape(size, part)
    near = [d for d in range(size) if min(d, size - d) <= size // 4 and d != size // 4]
    groups = [near, [d for d in range(size) if d not in near]]
    rows = [d for group in groups for d in group]
    x_parts = [tokens] + [None] * (size - 1)
    dy_parts = [cotangent] + [None] * (size - 1)
    acts = [[None, None] for _ in range(slots)]
    grads, back = [None] * slots, [None] * slots

    def pick(turn):
        return line.step(lambda after: pick_pass([turn], stride, fetch_pick, panels, after))[0]

    def make_acts(turn, g):
        take = groups[g]
        acts[turn][g] = line.step(
            lambda after: acts_pass(
                "nf"[g],
                turn,
                slots,
                stride,
                take,
                [x_parts[d] for d in take],
                [dy_parts[d] for d in take],
                read[turn],
                ring_routes,
                ring_weight,
                after,
            )
        )

    def make_grads(turn):
        shape = read[turn].shape
        grads[turn] = line.step(
            lambda after: grads_pass(
                turn,
                [x_parts[d] for d in rows],
                [dy_parts[d] for d in rows],
                acts[turn],
                [shape[1:]] * shape[0] if turn in middle else [shape],
                after,
            )
        )
        if turn != last:
            back[turn] = [exchange(grad, turn, slots) if turn else grad for grad in grads[turn]]

    read = [None] * slots
    read[late] = exchange(pick(late), late, slots)
    for turn in middle:
        read[turn] = exchange(pick(turn), turn, slots)
    read[last], read[0] = pick(last), pick(0)

    chains = [(x_parts, 1, up_most), (dy_parts, -1, up_most), (x_parts, -1, down_most), (dy_parts, 1, down_most)]
    moving = [ring_step(parts[0], order, way) for parts, way, _ in chains]
    for turn in middle:
        read[turn] = line.arrive(read[turn])
    for hop in range(1, up_most + 1):
        for i, (parts, way, hops) in enumerate(chains):
            if hop > hops:
                continue
            if hop == max(1, up_most // 2) and i == 2:
                read[late] = line.arrive(read[late])
                read[last] = exchange(line.arrive(read[last]), last, slots)
            arrived = line.arrive(moving[i])
            parts[-way * hop % size] = arrived
            if hop < hops:
                moving[i] = ring_step(arrived, order, way)
            if hop == max(1, up_most // 2) and i == len(chains) - 1:
                for turn in middle + [0]:
                    make_acts(turn, 0)

    for turn in middle:
        make_acts(turn, 1)
        make_grads(turn)
    make_acts(late, 0)
    make_acts(late, 1)
    make_grads(late)
    make_acts(0, 1)
    for turn in middle:
        back[turn] = [line.arrive(grad) for grad in back[turn]]
    read[last] = line.arrive(read[last])
    make_acts(last, 1)
    make_acts(last, 0)

    kinds = ("mixed", "grad")
    early = [("mixed", up_most), ("grad", size - up_most), ("mixed", size - down_most), ("grad", down_most)]
    early_cost = work_cost(6 * len(early) * slots * part * read[0].size // 6)
    later = [(kind, d) for kind in kinds for d in range(size) if (kind, d) not in early]
    chunks = dict(zip(early, line.step(lambda after: chunk_pass(early, acts, read, groups, part, early_cost, after))))
    chains = [("mixed", 1, up_most), ("grad", -1, up_most), ("mixed", -1, down_most), ("grad", 1, down_most)]
    moving = [ring_step(chunks[kind, way * hops % size], order, way) for kind, way, hops in chains]
    chunks.update(zip(later, line.step(lambda after: chunk_pass(later, acts, read, groups, part, NO_COST, after))))
    make_grads(last)
    make_grads(0)

    sums = {}
    for hop in range(1, up_most + 1):
        for i, (kind, way, hops) in enumerate(chains):
            if hop > hops:
                continue
            if hop == max(1, up_most // 2) and i == 2:
                back[late] = [line.arrive(back[late][0])]
                back[last] = exchange(line.arrive(grads[last][0]), last, slots)
            left = hops - hop
            if left:
                chunk = chunks[kind, way * left % size]
                arrived = line.step(lambda after: add_rows(moving[i], chunk, BF16, after))
                moving[i] = ring_step(arrived, order, way)
            elif kind not in sums:
                sums[kind] = line.step(lambda after: add_rows(moving[i], chunks[kind, 0], F32, after))
                if len(sums) == 2:
                    panel_grad, base, _ = line.step(
                        lambda after: total_pass(
                            list(range(last)), last, stride, fetch_pick, back[:last], panels.shape, after
                        )
                    )
            else:
                cost = work_cost(LAST_FLOPS) if (kind, hop) == (chains[1][0], up_most) else NO_COST
                sums[kind], _ = line.step(lambda after: final_rows(moving[i], sums[kind], cost, after))
    back[last] = line.arrive(back[last])
    panel_grad = add_pass(last, stride, fetch_pick, panel_grad, base, back[last])
    return sums["mixed"], sums["grad"], panel_grad


def solution(mesh):
    return jax.shard_map(
        body,
        mesh=mesh,
        in_specs=(
            P(("node", "local"), None),
            P(("node", "local"), None),
            P("node", None),
            P("node", None),
            P(),
            P("node", None, "local", None),
        ),
        out_specs=(
            P(("node", "local"), None),
            P(("node", "local"), None),
            P("node", None, "local", None),
        ),
        check_vma=False,
    )
```

```python
import jax
import jax.numpy as jnp
from jax import lax
from jax.experimental import pallas as pl
from jax.experimental.pallas import tpu as pltpu
from jax.sharding import PartitionSpec as P

BF16 = jnp.bfloat16
F32 = jnp.float32
VMEM_LIMIT = 24 * 1024 * 1024
NO_COST = pl.CostEstimate(flops=1, bytes_accessed=1, transcendentals=0)


LAST_FLOPS = 12 * 10**9


def work_cost(flops):
    return pl.CostEstimate(flops=flops, bytes_accessed=1, transcendentals=0)


CONTRACT_LAST = (((1,), (1,)), ((), ()))
CONTRACT_FIRST = (((0,), (0,)), ((), ()))


def whole_in_vmem():
    return pl.BlockSpec(memory_space=pltpu.VMEM)


def in_hbm():
    return pl.BlockSpec(memory_space=pltpu.HBM)


def token_shape():
    return jax.ShapeDtypeStruct((8, 128), F32)


def untouched():
    return pl.BlockSpec(memory_space=pl.ANY)


def tile_of(size, most):
    tile = min(size, most)
    while size % tile:
        tile -= 1
    return tile


def ring_order(size):
    return list(range(0, size, 2)) + list(range(1, size, 2))[::-1]


def ring_source(size, ahead):
    me = lax.axis_index("local")
    half = lax.div(size + 1, 2)
    place = jnp.where(lax.rem(me, 2) == 0, lax.div(me, 2), size - 1 - lax.div(me, 2))
    there = lax.rem(place + ahead, size)
    return jnp.where(there < half, 2 * there, 2 * (size - 1 - there) + 1)


def partner_of(place, turn, slots):
    return place ^ turn


def owner_of(node, turn, slots, stride):
    return partner_of(node // stride, turn, slots) * stride + node % stride


def turn_slot(turn, slots, stride):
    place = lax.div(lax.axis_index("node"), stride)
    return lax.rem(place - partner_of(place, turn, slots) + slots, slots)


def turn_pick(fetch_pick, turn, stride):
    slots = fetch_pick.shape[1]
    node = lax.axis_index("node")
    place = lax.div(node, stride)
    partner = partner_of(place, turn, slots)
    reader = partner * stride + lax.rem(node, stride)
    return fetch_pick[reader, lax.rem(partner - place + slots, slots)]


def exchange(block, turn, slots):
    size = lax.axis_size("node")
    stride = size // slots
    return lax.ppermute(
        block, "node", [(owner_of(node, turn, slots, stride), node) for node in range(size)]
    )


def pick_kernel(turns, stride, fetch_pick, panels, *refs):
    outs, sems = refs[-len(turns) - 1 : -1], refs[-1]
    copies = [
        pltpu.make_async_copy(panels.at[turn_pick(fetch_pick, turn, stride)], out, sems.at[i])
        for i, (turn, out) in enumerate(zip(turns, outs))
    ]
    for copy in copies:
        copy.start()
    for copy in copies:
        copy.wait()


def pick_pass(turns, stride, fetch_pick, panels, after=()):
    return pl.pallas_call(
        lambda *refs: pick_kernel(turns, stride, *refs),
        out_shape=tuple(jax.ShapeDtypeStruct(panels.shape[1:], BF16) for _ in turns),
        in_specs=[pl.BlockSpec(memory_space=pltpu.SMEM), in_hbm()] + [untouched()] * len(after),
        out_specs=tuple(untouched() for _ in turns),
        scratch_shapes=[pltpu.SemaphoreType.DMA((len(turns),))],
        compiler_params=pltpu.CompilerParams(vmem_limit_bytes=1024 * 1024),
        cost_estimate=NO_COST,
        name="pick",
    )(fetch_pick, panels, *after)


def gate(value, after):
    return pl.pallas_call(
        lambda *refs: None,
        out_shape=jax.ShapeDtypeStruct(value.shape, value.dtype),
        in_specs=[untouched()] * (1 + len(after)),
        out_specs=untouched(),
        input_output_aliases={0: 0},
        compiler_params=pltpu.CompilerParams(vmem_limit_bytes=1024 * 1024),
        cost_estimate=NO_COST,
        name="gate",
    )(value, *after)


def total_kernel(turns, last, stride, counts, fetch_pick, *refs):
    out, base, token, refs = *refs[-3:], list(refs[: sum(counts)])
    picks = [turn_pick(fetch_pick, turn, stride) for turn in turns]
    last_pick = turn_pick(fetch_pick, last, stride)
    token[...] = jnp.zeros_like(token)
    experts, kinds = out.shape[:2]
    grads = []
    for count in counts:
        taken, refs = refs[:count], refs[count:]
        grads.append([taken[0].at[kind] for kind in range(kinds)] if count == 1 else taken)
    for kind in range(kinds):
        terms = [grad[kind][...].astype(F32) for grad in grads]
        for e in range(experts):
            total = jnp.zeros(terms[0].shape, F32)
            for pick, term in zip(picks, terms):
                total += jnp.where(pick == e, term, 0.0)
            total = total.astype(BF16)
            out[e, kind] = total
            if e == 0:
                base[kind] = total
            else:

                @pl.when(last_pick == e)
                def _():
                    base[kind] = total


def total_pass(turns, last, stride, fetch_pick, grads, shape, after):
    counts = [len(grad) for grad in grads]
    return pl.pallas_call(
        lambda *refs: total_kernel(turns, last, stride, counts, *refs),
        out_shape=(
            jax.ShapeDtypeStruct(shape, BF16),
            jax.ShapeDtypeStruct(shape[1:], BF16),
            token_shape(),
        ),
        in_specs=[pl.BlockSpec(memory_space=pltpu.SMEM)]
        + [whole_in_vmem()] * sum(counts)
        + [untouched()] * len(after),
        out_specs=(whole_in_vmem(),) * 3,
        compiler_params=pltpu.CompilerParams(vmem_limit_bytes=VMEM_LIMIT),
        cost_estimate=NO_COST,
        name="total",
    )(fetch_pick, *[grad for slot_grads in grads for grad in slot_grads], *after)


def add_kernel(turn, stride, fetch_pick, total, base, grad, out, sums, sems):
    pick = turn_pick(fetch_pick, turn, stride)
    writes = [
        pltpu.make_async_copy(sums.at[kind], out.at[pick, kind], sems.at[kind])
        for kind in range(grad.shape[0])
    ]
    for kind, write in enumerate(writes):
        sums[kind] = (base[kind].astype(F32) + grad[kind].astype(F32)).astype(BF16)
        write.start()
    for write in writes:
        write.wait()


def add_pass(turn, stride, fetch_pick, total, base, grad):
    return pl.pallas_call(
        lambda *refs: add_kernel(turn, stride, *refs),
        out_shape=jax.ShapeDtypeStruct(total.shape, BF16),
        in_specs=[pl.BlockSpec(memory_space=pltpu.SMEM), in_hbm(), whole_in_vmem(), whole_in_vmem()],
        out_specs=in_hbm(),
        input_output_aliases={1: 0},
        scratch_shapes=[pltpu.VMEM(grad.shape, BF16), pltpu.SemaphoreType.DMA((grad.shape[0],))],
        compiler_params=pltpu.CompilerParams(vmem_limit_bytes=12 * 1024 * 1024),
        cost_estimate=NO_COST,
        name="add",
    )(fetch_pick, total, base, grad)


def ring_step(block, order, distance):
    size = len(order)
    return lax.ppermute(
        block, "local", [(order[i], order[(i + distance) % size]) for i in range(size)]
    )


def add_rows_kernel(*refs):
    a, b, out = refs[0], refs[1], refs[-1]
    out[...] = (a[...].astype(F32) + b[...].astype(F32)).astype(out.dtype)


def add_rows(a, b, dtype, after=()):
    return pl.pallas_call(
        add_rows_kernel,
        out_shape=jax.ShapeDtypeStruct(a.shape, dtype),
        in_specs=[whole_in_vmem()] * 2 + [untouched()] * len(after),
        out_specs=whole_in_vmem(),
        compiler_params=pltpu.CompilerParams(vmem_limit_bytes=VMEM_LIMIT),
        cost_estimate=NO_COST,
        name="add_rows",
    )(a, b, *after)


def acts_kernel(turn, slots, stride, size, offsets, *refs):
    parts = len(offsets)
    x_refs, dy_refs = refs[:parts], refs[parts : 2 * parts]
    panel, routes, weight, acts = *refs[2 * parts : 2 * parts + 3], refs[-1]
    units, width = panel.shape[1:]
    part = x_refs[0].shape[0]
    at_once = 2 if parts % 2 == 0 else 1
    slot = turn_slot(turn, slots, stride)
    for d in range(0, parts, at_once):
        here = slice(d * part, (d + at_once) * part)
        x = jnp.concatenate([ref[...] for ref in x_refs[d : d + at_once]], axis=0)
        dy = jnp.concatenate([ref[...] for ref in dy_refs[d : d + at_once]], axis=0)
        both = lax.dot_general(
            panel[0:2].reshape(2 * units, width), x, CONTRACT_LAST, preferred_element_type=F32
        )
        gate, up = both[:units], both[units:]
        d_hidden = lax.dot_general(panel[2], dy, CONTRACT_LAST, preferred_element_type=F32)
        sources = [ring_source(size, ahead) for ahead in offsets[d : d + at_once]]
        scale = jnp.concatenate(
            [
                jnp.where(routes[pl.ds(i, 1), :] == slot, weight[pl.ds(i, 1), :], 0.0)
                for i in sources
            ],
            axis=1,
        )
        sigmoid_gate = jax.nn.sigmoid(gate)
        activated = gate * sigmoid_gate
        d_hidden = d_hidden * scale
        d_gate = d_hidden * up * sigmoid_gate * (1.0 + gate * (1.0 - sigmoid_gate))
        acts[0:units, here] = d_gate.astype(BF16)
        acts[units : 2 * units, here] = (d_hidden * activated).astype(BF16)
        acts[2 * units : 3 * units, here] = (activated * up * scale).astype(BF16)


def acts_pass(name, turn, slots, stride, offsets, x_parts, dy_parts, panel, routes, weight, after=()):
    parts = len(x_parts)
    part = x_parts[0].shape[0]
    return pl.pallas_call(
        lambda *refs: acts_kernel(turn, slots, stride, routes.shape[0], offsets, *refs),
        out_shape=jax.ShapeDtypeStruct((3 * panel.shape[1], parts * part), BF16),
        in_specs=[whole_in_vmem()] * (2 * parts + 3) + [untouched()] * len(after),
        out_specs=whole_in_vmem(),
        compiler_params=pltpu.CompilerParams(vmem_limit_bytes=VMEM_LIMIT),
        cost_estimate=work_cost(6 * parts * part * panel.shape[1] * panel.shape[2]),
        name=f"acts_{turn}_{name}",
    )(*x_parts, *dy_parts, panel, routes, weight, *after)


def grads_kernel(parts, groups, kinds, *refs):
    x_refs, dy_refs = refs[:parts], refs[parts : 2 * parts]
    acts, grads = refs[2 * parts : 2 * parts + groups], refs[-kinds:]
    if kinds == 1:
        grads = [grads[0].at[kind] for kind in range(3)]
    units, width = grads[0].shape
    columns = tile_of(width, 512)
    for start in range(0, width, columns):
        here = slice(start, start + columns)
        x = jnp.concatenate([ref[:, here] for ref in x_refs], axis=0)
        dy = jnp.concatenate([ref[:, here] for ref in dy_refs], axis=0)
        d_both = jnp.concatenate([act[0 : 2 * units, :] for act in acts], axis=1)
        d_both = jnp.dot(d_both, x, preferred_element_type=F32).astype(BF16)
        grads[0][:, here] = d_both[0:units]
        grads[1][:, here] = d_both[units:]
        hidden = jnp.concatenate([act[2 * units : 3 * units, :] for act in acts], axis=1)
        grads[2][:, here] = jnp.dot(hidden, dy, preferred_element_type=F32).astype(BF16)


def grads_pass(turn, x_parts, dy_parts, acts, shapes, after=()):
    parts = len(x_parts)
    return pl.pallas_call(
        lambda *refs: grads_kernel(parts, len(acts), len(shapes), *refs),
        out_shape=tuple(jax.ShapeDtypeStruct(shape, BF16) for shape in shapes),
        in_specs=[whole_in_vmem()] * (2 * parts + len(acts)) + [untouched()] * len(after),
        out_specs=tuple(whole_in_vmem() for _ in shapes),
        compiler_params=pltpu.CompilerParams(vmem_limit_bytes=VMEM_LIMIT),
        cost_estimate=work_cost(6 * parts * acts[0].shape[0] // 3 * x_parts[0].size),
        name=f"grads_{turn}",
    )(*x_parts, *dy_parts, *acts, *after)


def chunk_kernel(wanted, slots, part, acts, panels, outs):
    units, width = panels[0].shape[1:]
    columns = tile_of(width, 512)

    @pl.loop(0, width // columns)
    def _(step):
        here = pl.ds(pl.multiple_of(step * columns, columns), columns)
        kinds = {"mixed": (2, 3), "grad": (0, 2)}
        sides = {
            kind: jnp.concatenate(
                [panel[which, :, here] for panel in panels for which in range(*span)], axis=0
            )
            for kind, span in kinds.items()
        }
        for out, (kind, group, row) in zip(outs, wanted):
            low, high = (units * which for which in kinds[kind])
            act = jnp.concatenate(
                [act[group][low:high, row * part : (row + 1) * part] for act in acts], axis=0
            )
            total = lax.dot_general(act, sides[kind], CONTRACT_FIRST, preferred_element_type=F32)
            out[:, here] = total.astype(BF16)


def chunk_pass(wanted, acts, panels, groups, part, cost, after=()):
    slots = len(panels)
    width = panels[0].shape[2]
    named = [
        (kind, g, group.index(d)) for kind, d in wanted for g, group in enumerate(groups) if d in group
    ]

    def kernel(*refs):
        act_refs = [refs[s * len(groups) : (s + 1) * len(groups)] for s in range(slots)]
        rest = refs[slots * len(groups) :]
        chunk_kernel(named, slots, part, act_refs, rest[:slots], rest[slots + len(after) :])

    return pl.pallas_call(
        kernel,
        out_shape=tuple(jax.ShapeDtypeStruct((part, width), BF16) for _ in wanted),
        in_specs=[whole_in_vmem()] * (slots * len(groups) + slots) + [untouched()] * len(after),
        out_specs=tuple(whole_in_vmem() for _ in wanted),
        compiler_params=pltpu.CompilerParams(vmem_limit_bytes=VMEM_LIMIT),
        cost_estimate=cost,
        name=f"chunks_{len(wanted)}",
    )(*[act for slot_acts in acts for act in slot_acts], *panels, *after)


def final_rows_kernel(*refs):
    a, b, out, token = refs[0], refs[1], *refs[-2:]
    out[...] = (a[...].astype(F32) + b[...]).astype(out.dtype)
    token[...] = jnp.zeros_like(token)


def final_rows(a, b, cost, after):
    return pl.pallas_call(
        final_rows_kernel,
        out_shape=(jax.ShapeDtypeStruct(a.shape, BF16), token_shape()),
        in_specs=[whole_in_vmem()] * 2 + [untouched()] * len(after),
        out_specs=(whole_in_vmem(), whole_in_vmem()),
        compiler_params=pltpu.CompilerParams(vmem_limit_bytes=VMEM_LIMIT),
        cost_estimate=cost,
        name="final_rows",
    )(a, b, *after)


class Line:
    def __init__(self):
        self.tail = ()

    def step(self, make):
        out = make(self.tail)
        self.tail = (out[-1] if isinstance(out, (tuple, list)) else out,)
        return out

    def arrive(self, value):
        return self.step(lambda after: gate(value, after))


def body(tokens, cotangent, routes, route_weight, fetch_pick, panels):
    panels = pltpu.with_memory_space_constraint(panels, pltpu.HBM)
    slots = fetch_pick.shape[1]
    stride = lax.axis_size("node") // slots
    part, width = tokens.shape
    order = ring_order(lax.axis_size("local"))
    size = len(order)
    up_most, down_most = size // 2, size - 1 - size // 2
    last, late = slots - 1, slots - 2
    middle = list(range(1, late))
    line = Line()

    ring_routes = routes.reshape(size, part)
    ring_weight = route_weight.reshape(size, part)
    near = [d for d in range(size) if min(d, size - d) <= size // 4 and d != size // 4]
    groups = [near, [d for d in range(size) if d not in near]]
    rows = [d for group in groups for d in group]
    x_parts = [tokens] + [None] * (size - 1)
    dy_parts = [cotangent] + [None] * (size - 1)
    acts = [[None, None] for _ in range(slots)]
    grads, back = [None] * slots, [None] * slots

    def make_acts(turn, g):
        take = groups[g]
        acts[turn][g] = line.step(
            lambda after: acts_pass(
                "nf"[g],
                turn,
                slots,
                stride,
                take,
                [x_parts[d] for d in take],
                [dy_parts[d] for d in take],
                read[turn],
                ring_routes,
                ring_weight,
                after,
            )
        )

    def make_grads(turn):
        shape = read[turn].shape
        grads[turn] = line.step(
            lambda after: grads_pass(
                turn,
                [x_parts[d] for d in rows],
                [dy_parts[d] for d in rows],
                acts[turn],
                [shape[1:]] * shape[0] if turn in middle else [shape],
                after,
            )
        )
        if turn != last:
            back[turn] = [exchange(grad, turn, slots) if turn else grad for grad in grads[turn]]

    read = [None] * slots
    first_turns = [late] + middle
    picked = line.step(lambda after: pick_pass(first_turns, stride, fetch_pick, panels, after))
    for turn, panel in zip(first_turns, picked):
        read[turn] = exchange(panel, turn, slots)
    read[last], read[0] = line.step(lambda after: pick_pass([last, 0], stride, fetch_pick, panels, after))

    chains = [(x_parts, 1, up_most), (dy_parts, -1, up_most), (x_parts, -1, down_most), (dy_parts, 1, down_most)]
    moving = [ring_step(parts[0], order, way) for parts, way, _ in chains]
    for turn in middle:
        read[turn] = line.arrive(read[turn])
    for hop in range(1, up_most + 1):
        for i, (parts, way, hops) in enumerate(chains):
            if hop > hops:
                continue
            if hop == max(1, up_most // 2) and i == 2:
                read[late] = line.arrive(read[late])
                read[last] = exchange(line.arrive(read[last]), last, slots)
            arrived = line.arrive(moving[i])
            parts[-way * hop % size] = arrived
            if hop < hops:
                moving[i] = ring_step(arrived, order, way)
            if hop == max(1, up_most // 2) and i == len(chains) - 1:
                for turn in middle + [0]:
                    make_acts(turn, 0)

    for turn in middle:
        make_acts(turn, 1)
        make_grads(turn)
    make_acts(late, 0)
    make_acts(late, 1)
    make_grads(late)
    make_acts(0, 1)
    for turn in middle:
        back[turn] = [line.arrive(grad) for grad in back[turn]]
    read[last] = line.arrive(read[last])
    make_acts(last, 1)
    make_acts(last, 0)

    kinds = ("mixed", "grad")
    early = [("mixed", up_most), ("grad", size - up_most), ("mixed", size - down_most), ("grad", down_most)]
    early_cost = work_cost(6 * len(early) * slots * part * read[0].size // 6)
    later = [(kind, d) for kind in kinds for d in range(size) if (kind, d) not in early]
    chunks = dict(zip(early, line.step(lambda after: chunk_pass(early, acts, read, groups, part, early_cost, after))))
    chains = [("mixed", 1, up_most), ("grad", -1, up_most), ("mixed", -1, down_most), ("grad", 1, down_most)]
    moving = [ring_step(chunks[kind, way * hops % size], order, way) for kind, way, hops in chains]
    chunks.update(zip(later, line.step(lambda after: chunk_pass(later, acts, read, groups, part, NO_COST, after))))
    make_grads(last)
    make_grads(0)

    sums = {}
    for hop in range(1, up_most + 1):
        for i, (kind, way, hops) in enumerate(chains):
            if hop > hops:
                continue
            if hop == max(1, up_most // 2) and i == 2:
                back[late] = [line.arrive(back[late][0])]
                back[last] = exchange(line.arrive(grads[last][0]), last, slots)
            left = hops - hop
            if left:
                chunk = chunks[kind, way * left % size]
                arrived = line.step(lambda after: add_rows(moving[i], chunk, BF16, after))
                moving[i] = ring_step(arrived, order, way)
            elif kind not in sums:
                sums[kind] = line.step(lambda after: add_rows(moving[i], chunks[kind, 0], F32, after))
                if len(sums) == 2:
                    panel_grad, base, _ = line.step(
                        lambda after: total_pass(
                            list(range(last)), last, stride, fetch_pick, back[:last], panels.shape, after
                        )
                    )
            else:
                cost = work_cost(LAST_FLOPS) if (kind, hop) == (chains[1][0], up_most) else NO_COST
                sums[kind], _ = line.step(lambda after: final_rows(moving[i], sums[kind], cost, after))
    back[last] = line.arrive(back[last])
    panel_grad = add_pass(last, stride, fetch_pick, panel_grad, base, back[last])
    return sums["mixed"], sums["grad"], panel_grad


def solution(mesh):
    return jax.shard_map(
        body,
        mesh=mesh,
        in_specs=(
            P(("node", "local"), None),
            P(("node", "local"), None),
            P("node", None),
            P("node", None),
            P(),
            P("node", None, "local", None),
        ),
        out_specs=(
            P(("node", "local"), None),
            P(("node", "local"), None),
            P("node", None, "local", None),
        ),
        check_vma=False,
    )
```

```python
import jax
import jax.numpy as jnp
from jax import lax
from jax.experimental import pallas as pl
from jax.experimental.pallas import tpu as pltpu
from jax.sharding import PartitionSpec as P

BF16 = jnp.bfloat16
F32 = jnp.float32
VMEM_LIMIT = 24 * 1024 * 1024
NO_COST = pl.CostEstimate(flops=1, bytes_accessed=1, transcendentals=0)


LAST_FLOPS = 12 * 10**9


def work_cost(flops):
    return pl.CostEstimate(flops=flops, bytes_accessed=1, transcendentals=0)


CONTRACT_LAST = (((1,), (1,)), ((), ()))
CONTRACT_FIRST = (((0,), (0,)), ((), ()))


def whole_in_vmem():
    return pl.BlockSpec(memory_space=pltpu.VMEM)


def in_hbm():
    return pl.BlockSpec(memory_space=pltpu.HBM)


def token_shape():
    return jax.ShapeDtypeStruct((8, 128), F32)


def by_kind(refs):
    return [refs[0].at[kind] for kind in range(3)] if len(refs) == 1 else list(refs)


def untouched():
    return pl.BlockSpec(memory_space=pl.ANY)


def tile_of(size, most):
    tile = min(size, most)
    while size % tile:
        tile -= 1
    return tile


def ring_order(size):
    return list(range(0, size, 2)) + list(range(1, size, 2))[::-1]


def ring_source(size, ahead):
    me = lax.axis_index("local")
    half = lax.div(size + 1, 2)
    place = jnp.where(lax.rem(me, 2) == 0, lax.div(me, 2), size - 1 - lax.div(me, 2))
    there = lax.rem(place + ahead, size)
    return jnp.where(there < half, 2 * there, 2 * (size - 1 - there) + 1)


def partner_of(place, turn, slots):
    return place ^ turn


def owner_of(node, turn, slots, stride):
    return partner_of(node // stride, turn, slots) * stride + node % stride


def turn_slot(turn, slots, stride):
    place = lax.div(lax.axis_index("node"), stride)
    return lax.rem(place - partner_of(place, turn, slots) + slots, slots)


def turn_pick(fetch_pick, turn, stride):
    slots = fetch_pick.shape[1]
    node = lax.axis_index("node")
    place = lax.div(node, stride)
    partner = partner_of(place, turn, slots)
    reader = partner * stride + lax.rem(node, stride)
    return fetch_pick[reader, lax.rem(partner - place + slots, slots)]


def exchange(block, turn, slots):
    size = lax.axis_size("node")
    stride = size // slots
    return lax.ppermute(
        block, "node", [(owner_of(node, turn, slots, stride), node) for node in range(size)]
    )


def halves(units):
    middle = max(16, units // 32 * 16) if units > 16 else units
    return [(0, middle), (middle, units)] if middle < units else [(0, units)]


def pick_kernel(turns, stride, apart, fetch_pick, panels, *refs):
    kinds, units = panels.shape[1:3]
    spans = halves(units)
    outs, sems = refs[-len(turns) * (kinds if apart else 1) - 1 : -1], refs[-1]
    copies = []
    for i, turn in enumerate(turns):
        pick = turn_pick(fetch_pick, turn, stride)
        for kind in range(kinds):
            out = outs[i * kinds + kind] if apart else outs[i].at[kind]
            for j, (low, high) in enumerate(spans):
                here = pl.ds(low, high - low)
                copies.append(
                    pltpu.make_async_copy(
                        panels.at[pick, kind, here], out.at[here], sems.at[i, kind, j]
                    )
                )
    for copy in copies:
        copy.start()
    for copy in copies:
        copy.wait()


def pick_pass(turns, stride, fetch_pick, panels, apart, after=()):
    kinds = panels.shape[1]
    shapes = [panels.shape[2:]] * kinds if apart else [panels.shape[1:]]
    shapes = shapes * len(turns)
    out = pl.pallas_call(
        lambda *refs: pick_kernel(turns, stride, apart, *refs),
        out_shape=tuple(jax.ShapeDtypeStruct(shape, BF16) for shape in shapes),
        in_specs=[pl.BlockSpec(memory_space=pltpu.SMEM), in_hbm()] + [untouched()] * len(after),
        out_specs=tuple(untouched() for _ in shapes),
        scratch_shapes=[pltpu.SemaphoreType.DMA((len(turns), kinds, 2))],
        compiler_params=pltpu.CompilerParams(vmem_limit_bytes=1024 * 1024),
        cost_estimate=NO_COST,
        name="pick",
    )(fetch_pick, panels, *after)
    return out


def gate(value, after):
    return pl.pallas_call(
        lambda *refs: None,
        out_shape=jax.ShapeDtypeStruct(value.shape, value.dtype),
        in_specs=[untouched()] * (1 + len(after)),
        out_specs=untouched(),
        input_output_aliases={0: 0},
        compiler_params=pltpu.CompilerParams(vmem_limit_bytes=1024 * 1024),
        cost_estimate=NO_COST,
        name="gate",
    )(value, *after)


def total_kernel(turns, last, stride, counts, fetch_pick, *refs):
    out, base, token, refs = *refs[-3:], list(refs[: sum(counts)])
    picks = [turn_pick(fetch_pick, turn, stride) for turn in turns]
    last_pick = turn_pick(fetch_pick, last, stride)
    token[...] = jnp.zeros_like(token)
    experts, kinds = out.shape[:2]
    grads = []
    for count in counts:
        taken, refs = refs[:count], refs[count:]
        grads.append([taken[0].at[kind] for kind in range(kinds)] if count == 1 else taken)
    for kind in range(kinds):
        terms = [grad[kind][...].astype(F32) for grad in grads]
        for e in range(experts):
            total = jnp.zeros(terms[0].shape, F32)
            for pick, term in zip(picks, terms):
                total += jnp.where(pick == e, term, 0.0)
            total = total.astype(BF16)
            out[e, kind] = total
            if e == 0:
                base[kind] = total
            else:

                @pl.when(last_pick == e)
                def _():
                    base[kind] = total


def total_pass(turns, last, stride, fetch_pick, grads, shape, after):
    counts = [len(grad) for grad in grads]
    return pl.pallas_call(
        lambda *refs: total_kernel(turns, last, stride, counts, *refs),
        out_shape=(
            jax.ShapeDtypeStruct(shape, BF16),
            jax.ShapeDtypeStruct(shape[1:], BF16),
            token_shape(),
        ),
        in_specs=[pl.BlockSpec(memory_space=pltpu.SMEM)]
        + [whole_in_vmem()] * sum(counts)
        + [untouched()] * len(after),
        out_specs=(whole_in_vmem(),) * 3,
        compiler_params=pltpu.CompilerParams(vmem_limit_bytes=VMEM_LIMIT),
        cost_estimate=NO_COST,
        name="total",
    )(fetch_pick, *[grad for slot_grads in grads for grad in slot_grads], *after)


def add_kernel(turn, stride, fetch_pick, total, base, grad, out, sums, sems):
    pick = turn_pick(fetch_pick, turn, stride)
    writes = []
    for kind in range(grad.shape[0]):
        for j, (low, high) in enumerate(halves(grad.shape[1])):
            here = pl.ds(low, high - low)
            sums[kind, here] = (base[kind, here].astype(F32) + grad[kind, here].astype(F32)).astype(BF16)
            write = pltpu.make_async_copy(
                sums.at[kind, here], out.at[pick, kind, here], sems.at[kind, j]
            )
            write.start()
            writes.append(write)
    for write in writes:
        write.wait()


def add_pass(turn, stride, fetch_pick, total, base, grad):
    return pl.pallas_call(
        lambda *refs: add_kernel(turn, stride, *refs),
        out_shape=jax.ShapeDtypeStruct(total.shape, BF16),
        in_specs=[pl.BlockSpec(memory_space=pltpu.SMEM), in_hbm(), whole_in_vmem(), whole_in_vmem()],
        out_specs=in_hbm(),
        input_output_aliases={1: 0},
        scratch_shapes=[pltpu.VMEM(grad.shape, BF16), pltpu.SemaphoreType.DMA((grad.shape[0], 2))],
        compiler_params=pltpu.CompilerParams(vmem_limit_bytes=12 * 1024 * 1024),
        cost_estimate=NO_COST,
        name="add",
    )(fetch_pick, total, base, grad)


def ring_step(block, order, distance):
    size = len(order)
    return lax.ppermute(
        block, "local", [(order[i], order[(i + distance) % size]) for i in range(size)]
    )


def add_rows_kernel(*refs):
    a, b, out = refs[0], refs[1], refs[-1]
    out[...] = (a[...].astype(F32) + b[...].astype(F32)).astype(out.dtype)


def add_rows(a, b, dtype, after=()):
    return pl.pallas_call(
        add_rows_kernel,
        out_shape=jax.ShapeDtypeStruct(a.shape, dtype),
        in_specs=[whole_in_vmem()] * 2 + [untouched()] * len(after),
        out_specs=whole_in_vmem(),
        compiler_params=pltpu.CompilerParams(vmem_limit_bytes=VMEM_LIMIT),
        cost_estimate=NO_COST,
        name="add_rows",
    )(a, b, *after)


def acts_kernel(turn, slots, stride, size, offsets, pieces, *refs):
    parts = len(offsets)
    x_refs, dy_refs = refs[:parts], refs[parts : 2 * parts]
    panel, (routes, weight), acts = by_kind(refs[2 * parts : 2 * parts + pieces]), refs[
        2 * parts + pieces : 2 * parts + pieces + 2
    ], refs[-1]
    units, width = panel[0].shape
    part = x_refs[0].shape[0]
    at_once = 2 if parts % 2 == 0 else 1
    slot = turn_slot(turn, slots, stride)
    for d in range(0, parts, at_once):
        here = slice(d * part, (d + at_once) * part)
        x = jnp.concatenate([ref[...] for ref in x_refs[d : d + at_once]], axis=0)
        dy = jnp.concatenate([ref[...] for ref in dy_refs[d : d + at_once]], axis=0)
        both = lax.dot_general(
            jnp.concatenate([panel[0][...], panel[1][...]], axis=0), x, CONTRACT_LAST, preferred_element_type=F32
        )
        gate, up = both[:units], both[units:]
        d_hidden = lax.dot_general(panel[2][...], dy, CONTRACT_LAST, preferred_element_type=F32)
        sources = [ring_source(size, ahead) for ahead in offsets[d : d + at_once]]
        scale = jnp.concatenate(
            [
                jnp.where(routes[pl.ds(i, 1), :] == slot, weight[pl.ds(i, 1), :], 0.0)
                for i in sources
            ],
            axis=1,
        )
        sigmoid_gate = jax.nn.sigmoid(gate)
        activated = gate * sigmoid_gate
        d_hidden = d_hidden * scale
        d_gate = d_hidden * up * sigmoid_gate * (1.0 + gate * (1.0 - sigmoid_gate))
        acts[0:units, here] = d_gate.astype(BF16)
        acts[units : 2 * units, here] = (d_hidden * activated).astype(BF16)
        acts[2 * units : 3 * units, here] = (activated * up * scale).astype(BF16)


def acts_pass(name, turn, slots, stride, offsets, x_parts, dy_parts, panel, routes, weight, after=()):
    parts = len(x_parts)
    part = x_parts[0].shape[0]
    return pl.pallas_call(
        lambda *refs: acts_kernel(
            turn, slots, stride, routes.shape[0], offsets, len(panel), *refs
        ),
        out_shape=jax.ShapeDtypeStruct((3 * panel[0].shape[-2], parts * part), BF16),
        in_specs=[whole_in_vmem()] * (2 * parts + len(panel) + 2) + [untouched()] * len(after),
        out_specs=whole_in_vmem(),
        compiler_params=pltpu.CompilerParams(vmem_limit_bytes=VMEM_LIMIT),
        cost_estimate=NO_COST,
        name=f"acts_{turn}_{name}",
    )(*x_parts, *dy_parts, *panel, routes, weight, *after)


def grads_kernel(parts, groups, kinds, *refs):
    x_refs, dy_refs = refs[:parts], refs[parts : 2 * parts]
    acts, grads = refs[2 * parts : 2 * parts + groups], refs[-kinds:]
    if kinds == 1:
        grads = [grads[0].at[kind] for kind in range(3)]
    units, width = grads[0].shape
    columns = tile_of(width, 512)
    for start in range(0, width, columns):
        here = slice(start, start + columns)
        x = jnp.concatenate([ref[:, here] for ref in x_refs], axis=0)
        dy = jnp.concatenate([ref[:, here] for ref in dy_refs], axis=0)
        d_both = jnp.concatenate([act[0 : 2 * units, :] for act in acts], axis=1)
        d_both = jnp.dot(d_both, x, preferred_element_type=F32).astype(BF16)
        grads[0][:, here] = d_both[0:units]
        grads[1][:, here] = d_both[units:]
        hidden = jnp.concatenate([act[2 * units : 3 * units, :] for act in acts], axis=1)
        grads[2][:, here] = jnp.dot(hidden, dy, preferred_element_type=F32).astype(BF16)


def grads_pass(turn, x_parts, dy_parts, acts, shapes, after=()):
    parts = len(x_parts)
    return pl.pallas_call(
        lambda *refs: grads_kernel(parts, len(acts), len(shapes), *refs),
        out_shape=tuple(jax.ShapeDtypeStruct(shape, BF16) for shape in shapes),
        in_specs=[whole_in_vmem()] * (2 * parts + len(acts)) + [untouched()] * len(after),
        out_specs=tuple(whole_in_vmem() for _ in shapes),
        compiler_params=pltpu.CompilerParams(vmem_limit_bytes=VMEM_LIMIT),
        cost_estimate=work_cost(6 * parts * acts[0].shape[0] // 3 * x_parts[0].size),
        name=f"grads_{turn}",
    )(*x_parts, *dy_parts, *acts, *after)


def chunk_kernel(wanted, slots, part, acts, panels, outs):
    units, width = panels[0][0].shape
    columns = tile_of(width, 512)

    @pl.loop(0, width // columns)
    def _(step):
        here = pl.ds(pl.multiple_of(step * columns, columns), columns)
        kinds = {"mixed": (2, 3), "grad": (0, 2)}
        sides = {
            kind: jnp.concatenate(
                [panel[which][:, here] for panel in panels for which in range(*span)], axis=0
            )
            for kind, span in kinds.items()
        }
        for out, (kind, group, row) in zip(outs, wanted):
            low, high = (units * which for which in kinds[kind])
            act = jnp.concatenate(
                [act[group][low:high, row * part : (row + 1) * part] for act in acts], axis=0
            )
            total = lax.dot_general(act, sides[kind], CONTRACT_FIRST, preferred_element_type=F32)
            out[:, here] = total.astype(BF16)


def chunk_pass(wanted, acts, panels, groups, part, cost, after=()):
    slots = len(panels)
    width = panels[0][0].shape[-1]
    pieces = [len(panel) for panel in panels]
    named = [
        (kind, g, group.index(d)) for kind, d in wanted for g, group in enumerate(groups) if d in group
    ]

    def kernel(*refs):
        act_refs = [refs[s * len(groups) : (s + 1) * len(groups)] for s in range(slots)]
        rest = refs[slots * len(groups) :]
        starts = [sum(pieces[:s]) for s in range(slots)]
        panel_refs = [by_kind(rest[a : a + n]) for a, n in zip(starts, pieces)]
        chunk_kernel(named, slots, part, act_refs, panel_refs, rest[sum(pieces) + len(after) :])

    return pl.pallas_call(
        kernel,
        out_shape=tuple(jax.ShapeDtypeStruct((part, width), BF16) for _ in wanted),
        in_specs=[whole_in_vmem()] * (slots * len(groups) + sum(pieces)) + [untouched()] * len(after),
        out_specs=tuple(whole_in_vmem() for _ in wanted),
        compiler_params=pltpu.CompilerParams(vmem_limit_bytes=VMEM_LIMIT),
        cost_estimate=cost,
        name=f"chunks_{len(wanted)}",
    )(*[act for slot_acts in acts for act in slot_acts], *[piece for panel in panels for piece in panel], *after)


def final_rows_kernel(*refs):
    a, b, out, token = refs[0], refs[1], *refs[-2:]
    out[...] = (a[...].astype(F32) + b[...]).astype(out.dtype)
    token[...] = jnp.zeros_like(token)


def final_rows(a, b, cost, after):
    return pl.pallas_call(
        final_rows_kernel,
        out_shape=(jax.ShapeDtypeStruct(a.shape, BF16), token_shape()),
        in_specs=[whole_in_vmem()] * 2 + [untouched()] * len(after),
        out_specs=(whole_in_vmem(), whole_in_vmem()),
        compiler_params=pltpu.CompilerParams(vmem_limit_bytes=VMEM_LIMIT),
        cost_estimate=cost,
        name="final_rows",
    )(a, b, *after)


class Line:
    def __init__(self):
        self.tail = ()

    def step(self, make):
        out = make(self.tail)
        self.tail = (out[-1] if isinstance(out, (tuple, list)) else out,)
        return out

    def arrive(self, value):
        return self.step(lambda after: gate(value, after))


def body(tokens, cotangent, routes, route_weight, fetch_pick, panels):
    panels = pltpu.with_memory_space_constraint(panels, pltpu.HBM)
    slots = fetch_pick.shape[1]
    stride = lax.axis_size("node") // slots
    part, width = tokens.shape
    order = ring_order(lax.axis_size("local"))
    size = len(order)
    up_most, down_most = size // 2, size - 1 - size // 2
    last, late = slots - 1, slots - 2
    middle = list(range(1, late))
    line = Line()

    ring_routes = routes.reshape(size, part)
    ring_weight = route_weight.reshape(size, part)
    near = [d for d in range(size) if min(d, size - d) <= size // 4 and d != size // 4]
    groups = [near, [d for d in range(size) if d not in near]]
    rows = [d for group in groups for d in group]
    x_parts = [tokens] + [None] * (size - 1)
    dy_parts = [cotangent] + [None] * (size - 1)
    acts = [[None, None] for _ in range(slots)]
    grads, back = [None] * slots, [None] * slots

    def make_acts(turn, g):
        take = groups[g]
        acts[turn][g] = line.step(
            lambda after: acts_pass(
                "nf"[g],
                turn,
                slots,
                stride,
                take,
                [x_parts[d] for d in take],
                [dy_parts[d] for d in take],
                read[turn],
                ring_routes,
                ring_weight,
                after,
            )
        )

    def make_grads(turn):
        shape = panels.shape[1:]
        grads[turn] = line.step(
            lambda after: grads_pass(
                turn,
                [x_parts[d] for d in rows],
                [dy_parts[d] for d in rows],
                acts[turn],
                [shape[1:]] * shape[0] if turn in middle else [shape],
                after,
            )
        )
        if turn != last:
            back[turn] = [exchange(grad, turn, slots) if turn else grad for grad in grads[turn]]

    read = [None] * slots
    picked = line.step(lambda after: pick_pass([late], stride, fetch_pick, panels, False, after))
    read[late] = [exchange(picked[0], late, slots)]
    for turn in middle:
        picked = line.step(lambda after: pick_pass([turn], stride, fetch_pick, panels, True, after))
        read[turn] = [exchange(piece, turn, slots) for piece in picked]
    picked = line.step(lambda after: pick_pass([last, 0], stride, fetch_pick, panels, False, after))
    read[last], read[0] = [[piece] for piece in picked]

    chains = [(x_parts, 1, up_most), (dy_parts, -1, up_most), (x_parts, -1, down_most), (dy_parts, 1, down_most)]
    moving = [ring_step(parts[0], order, way) for parts, way, _ in chains]
    for turn in middle:
        read[turn] = [line.arrive(piece) for piece in read[turn]]
    for hop in range(1, up_most + 1):
        for i, (parts, way, hops) in enumerate(chains):
            if hop > hops:
                continue
            if hop == max(1, up_most // 2) and i == 2:
                read[late] = [line.arrive(read[late][0])]
                read[last] = [exchange(line.arrive(read[last][0]), last, slots)]
            arrived = line.arrive(moving[i])
            parts[-way * hop % size] = arrived
            if hop < hops:
                moving[i] = ring_step(arrived, order, way)
            if hop == max(1, up_most // 2) and i == len(chains) - 1:
                for turn in middle + [0, late]:
                    make_acts(turn, 0)

    make_acts(late, 1)
    make_grads(late)
    for turn in middle:
        make_acts(turn, 1)
        make_grads(turn)
    make_acts(0, 1)
    read[last] = [line.arrive(read[last][0])]
    make_acts(last, 1)
    make_acts(last, 0)
    for turn in middle:
        back[turn] = [line.arrive(grad) for grad in back[turn]]

    kinds = ("mixed", "grad")
    early = [("mixed", up_most), ("grad", size - up_most), ("mixed", size - down_most), ("grad", down_most)]
    early_cost = work_cost(6 * len(early) * slots * part * read[0][0].size // 6)
    later = [(kind, d) for kind in kinds for d in range(size) if (kind, d) not in early]
    chunks = dict(zip(early, line.step(lambda after: chunk_pass(early, acts, read, groups, part, early_cost, after))))
    chains = [("mixed", 1, up_most), ("grad", -1, up_most), ("mixed", -1, down_most), ("grad", 1, down_most)]
    moving = [ring_step(chunks[kind, way * hops % size], order, way) for kind, way, hops in chains]
    chunks.update(zip(later, line.step(lambda after: chunk_pass(later, acts, read, groups, part, NO_COST, after))))
    make_grads(last)
    make_grads(0)

    sums = {}
    for hop in range(1, up_most + 1):
        for i, (kind, way, hops) in enumerate(chains):
            if hop > hops:
                continue
            if hop == max(1, up_most // 2) and i == 2:
                back[late] = [line.arrive(back[late][0])]
                back[last] = exchange(line.arrive(grads[last][0]), last, slots)
            left = hops - hop
            if left:
                chunk = chunks[kind, way * left % size]
                arrived = line.step(lambda after: add_rows(moving[i], chunk, BF16, after))
                moving[i] = ring_step(arrived, order, way)
            elif kind not in sums:
                sums[kind] = line.step(lambda after: add_rows(moving[i], chunks[kind, 0], F32, after))
                if len(sums) == 2:
                    panel_grad, base, _ = line.step(
                        lambda after: total_pass(
                            list(range(last)), last, stride, fetch_pick, back[:last], panels.shape, after
                        )
                    )
            else:
                cost = work_cost(LAST_FLOPS) if (kind, hop) == (chains[1][0], up_most) else NO_COST
                sums[kind], _ = line.step(lambda after: final_rows(moving[i], sums[kind], cost, after))
    back[last] = line.arrive(back[last])
    panel_grad = add_pass(last, stride, fetch_pick, panel_grad, base, back[last])
    return sums["mixed"], sums["grad"], panel_grad


def solution(mesh):
    return jax.shard_map(
        body,
        mesh=mesh,
        in_specs=(
            P(("node", "local"), None),
            P(("node", "local"), None),
            P("node", None),
            P("node", None),
            P(),
            P("node", None, "local", None),
        ),
        out_specs=(
            P(("node", "local"), None),
            P(("node", "local"), None),
            P("node", None, "local", None),
        ),
        check_vma=False,
    )
```

```python
import jax
import jax.numpy as jnp
from jax import lax
from jax.experimental import pallas as pl
from jax.experimental.pallas import tpu as pltpu
from jax.sharding import PartitionSpec as P

BF16 = jnp.bfloat16
F32 = jnp.float32
VMEM_LIMIT = 24 * 1024 * 1024
NO_COST = pl.CostEstimate(flops=1, bytes_accessed=1, transcendentals=0)


LAST_FLOPS = 12 * 10**9


def work_cost(flops):
    return pl.CostEstimate(flops=flops, bytes_accessed=1, transcendentals=0)


CONTRACT_LAST = (((1,), (1,)), ((), ()))
CONTRACT_FIRST = (((0,), (0,)), ((), ()))


def whole_in_vmem():
    return pl.BlockSpec(memory_space=pltpu.VMEM)


def in_hbm():
    return pl.BlockSpec(memory_space=pltpu.HBM)


def token_shape():
    return jax.ShapeDtypeStruct((8, 128), F32)


def by_kind(refs):
    return [refs[0].at[kind] for kind in range(3)] if len(refs) == 1 else list(refs)


def untouched():
    return pl.BlockSpec(memory_space=pl.ANY)


def tile_of(size, most):
    tile = min(size, most)
    while size % tile:
        tile -= 1
    return tile


def ring_order(size):
    return list(range(0, size, 2)) + list(range(1, size, 2))[::-1]


def ring_source(size, ahead):
    me = lax.axis_index("local")
    half = lax.div(size + 1, 2)
    place = jnp.where(lax.rem(me, 2) == 0, lax.div(me, 2), size - 1 - lax.div(me, 2))
    there = lax.rem(place + ahead, size)
    return jnp.where(there < half, 2 * there, 2 * (size - 1 - there) + 1)


def partner_of(place, turn, slots):
    return place ^ turn


def owner_of(node, turn, slots, stride):
    return partner_of(node // stride, turn, slots) * stride + node % stride


def turn_slot(turn, slots, stride):
    place = lax.div(lax.axis_index("node"), stride)
    return lax.rem(place - partner_of(place, turn, slots) + slots, slots)


def turn_pick(fetch_pick, turn, stride):
    slots = fetch_pick.shape[1]
    node = lax.axis_index("node")
    place = lax.div(node, stride)
    partner = partner_of(place, turn, slots)
    reader = partner * stride + lax.rem(node, stride)
    return fetch_pick[reader, lax.rem(partner - place + slots, slots)]


def exchange(block, turn, slots):
    size = lax.axis_size("node")
    stride = size // slots
    return lax.ppermute(
        block, "node", [(owner_of(node, turn, slots, stride), node) for node in range(size)]
    )


def halves(units):
    middle = max(16, units // 32 * 16) if units > 16 else units
    return [(0, middle), (middle, units)] if middle < units else [(0, units)]


def pick_kernel(turns, stride, apart, fetch_pick, panels, *refs):
    kinds, units = panels.shape[1:3]
    spans = halves(units)
    outs, sems = refs[-len(turns) * (kinds if apart else 1) - 1 : -1], refs[-1]
    copies = []
    for i, turn in enumerate(turns):
        pick = turn_pick(fetch_pick, turn, stride)
        for kind in range(kinds):
            out = outs[i * kinds + kind] if apart else outs[i].at[kind]
            for j, (low, high) in enumerate(spans):
                here = pl.ds(low, high - low)
                copies.append(
                    pltpu.make_async_copy(
                        panels.at[pick, kind, here], out.at[here], sems.at[i, kind, j]
                    )
                )
    for copy in copies:
        copy.start()
    for copy in copies:
        copy.wait()


def pick_pass(turns, stride, fetch_pick, panels, apart, after=()):
    kinds = panels.shape[1]
    shapes = [panels.shape[2:]] * kinds if apart else [panels.shape[1:]]
    shapes = shapes * len(turns)
    out = pl.pallas_call(
        lambda *refs: pick_kernel(turns, stride, apart, *refs),
        out_shape=tuple(jax.ShapeDtypeStruct(shape, BF16) for shape in shapes),
        in_specs=[pl.BlockSpec(memory_space=pltpu.SMEM), in_hbm()] + [untouched()] * len(after),
        out_specs=tuple(untouched() for _ in shapes),
        scratch_shapes=[pltpu.SemaphoreType.DMA((len(turns), kinds, 2))],
        compiler_params=pltpu.CompilerParams(vmem_limit_bytes=1024 * 1024),
        cost_estimate=NO_COST,
        name="pick",
    )(fetch_pick, panels, *after)
    return out


def gate(value, after):
    return pl.pallas_call(
        lambda *refs: None,
        out_shape=jax.ShapeDtypeStruct(value.shape, value.dtype),
        in_specs=[untouched()] * (1 + len(after)),
        out_specs=untouched(),
        input_output_aliases={0: 0},
        compiler_params=pltpu.CompilerParams(vmem_limit_bytes=1024 * 1024),
        cost_estimate=NO_COST,
        name="gate",
    )(value, *after)


def total_kernel(turns, last, stride, counts, fetch_pick, *refs):
    out, base, token, refs = *refs[-3:], list(refs[: sum(counts)])
    picks = [turn_pick(fetch_pick, turn, stride) for turn in turns]
    last_pick = turn_pick(fetch_pick, last, stride)
    token[...] = jnp.zeros_like(token)
    experts, kinds = out.shape[:2]
    grads = []
    for count in counts:
        taken, refs = refs[:count], refs[count:]
        grads.append([taken[0].at[kind] for kind in range(kinds)] if count == 1 else taken)
    for kind in range(kinds):
        terms = [grad[kind][...].astype(F32) for grad in grads]
        for e in range(experts):
            total = jnp.zeros(terms[0].shape, F32)
            for pick, term in zip(picks, terms):
                total += jnp.where(pick == e, term, 0.0)
            total = total.astype(BF16)
            out[e, kind] = total
            if e == 0:
                base[kind] = total
            else:

                @pl.when(last_pick == e)
                def _():
                    base[kind] = total


def total_pass(turns, last, stride, fetch_pick, grads, shape, after):
    counts = [len(grad) for grad in grads]
    return pl.pallas_call(
        lambda *refs: total_kernel(turns, last, stride, counts, *refs),
        out_shape=(
            jax.ShapeDtypeStruct(shape, BF16),
            jax.ShapeDtypeStruct(shape[1:], BF16),
            token_shape(),
        ),
        in_specs=[pl.BlockSpec(memory_space=pltpu.SMEM)]
        + [whole_in_vmem()] * sum(counts)
        + [untouched()] * len(after),
        out_specs=(whole_in_vmem(),) * 3,
        compiler_params=pltpu.CompilerParams(vmem_limit_bytes=VMEM_LIMIT),
        cost_estimate=NO_COST,
        name="total",
    )(fetch_pick, *[grad for slot_grads in grads for grad in slot_grads], *after)


def add_kernel(turn, stride, fetch_pick, total, base, grad, out, sums, sems):
    pick = turn_pick(fetch_pick, turn, stride)
    writes = []
    for kind in range(grad.shape[0]):
        for j, (low, high) in enumerate(halves(grad.shape[1])):
            here = pl.ds(low, high - low)
            sums[kind, here] = (base[kind, here].astype(F32) + grad[kind, here].astype(F32)).astype(BF16)
            write = pltpu.make_async_copy(
                sums.at[kind, here], out.at[pick, kind, here], sems.at[kind, j]
            )
            write.start()
            writes.append(write)
    for write in writes:
        write.wait()


def add_pass(turn, stride, fetch_pick, total, base, grad):
    return pl.pallas_call(
        lambda *refs: add_kernel(turn, stride, *refs),
        out_shape=jax.ShapeDtypeStruct(total.shape, BF16),
        in_specs=[pl.BlockSpec(memory_space=pltpu.SMEM), in_hbm(), whole_in_vmem(), whole_in_vmem()],
        out_specs=in_hbm(),
        input_output_aliases={1: 0},
        scratch_shapes=[pltpu.VMEM(grad.shape, BF16), pltpu.SemaphoreType.DMA((grad.shape[0], 2))],
        compiler_params=pltpu.CompilerParams(vmem_limit_bytes=12 * 1024 * 1024),
        cost_estimate=NO_COST,
        name="add",
    )(fetch_pick, total, base, grad)


def ring_step(block, order, distance):
    size = len(order)
    return lax.ppermute(
        block, "local", [(order[i], order[(i + distance) % size]) for i in range(size)]
    )


def add_rows_kernel(*refs):
    a, b, out = refs[0], refs[1], refs[-1]
    out[...] = (a[...].astype(F32) + b[...].astype(F32)).astype(out.dtype)


def add_rows(a, b, dtype, after=()):
    return pl.pallas_call(
        add_rows_kernel,
        out_shape=jax.ShapeDtypeStruct(a.shape, dtype),
        in_specs=[whole_in_vmem()] * 2 + [untouched()] * len(after),
        out_specs=whole_in_vmem(),
        compiler_params=pltpu.CompilerParams(vmem_limit_bytes=VMEM_LIMIT),
        cost_estimate=NO_COST,
        name="add_rows",
    )(a, b, *after)


def acts_kernel(turn, slots, stride, size, offsets, pieces, *refs):
    parts = len(offsets)
    x_refs, dy_refs = refs[:parts], refs[parts : 2 * parts]
    panel, (routes, weight), acts = by_kind(refs[2 * parts : 2 * parts + pieces]), refs[
        2 * parts + pieces : 2 * parts + pieces + 2
    ], refs[-1]
    units, width = panel[0].shape
    part = x_refs[0].shape[0]
    at_once = 2 if parts % 2 == 0 else 1
    slot = turn_slot(turn, slots, stride)
    for d in range(0, parts, at_once):
        here = slice(d * part, (d + at_once) * part)
        x = jnp.concatenate([ref[...] for ref in x_refs[d : d + at_once]], axis=0)
        dy = jnp.concatenate([ref[...] for ref in dy_refs[d : d + at_once]], axis=0)
        both = lax.dot_general(
            jnp.concatenate([panel[0][...], panel[1][...]], axis=0), x, CONTRACT_LAST, preferred_element_type=F32
        )
        gate, up = both[:units], both[units:]
        d_hidden = lax.dot_general(panel[2][...], dy, CONTRACT_LAST, preferred_element_type=F32)
        sources = [ring_source(size, ahead) for ahead in offsets[d : d + at_once]]
        scale = jnp.concatenate(
            [
                jnp.where(routes[pl.ds(i, 1), :] == slot, weight[pl.ds(i, 1), :], 0.0)
                for i in sources
            ],
            axis=1,
        )
        sigmoid_gate = jax.nn.sigmoid(gate)
        activated = gate * sigmoid_gate
        d_hidden = d_hidden * scale
        d_gate = d_hidden * up * sigmoid_gate * (1.0 + gate * (1.0 - sigmoid_gate))
        acts[0:units, here] = d_gate.astype(BF16)
        acts[units : 2 * units, here] = (d_hidden * activated).astype(BF16)
        acts[2 * units : 3 * units, here] = (activated * up * scale).astype(BF16)


def acts_pass(name, turn, slots, stride, offsets, x_parts, dy_parts, panel, routes, weight, after=()):
    parts = len(x_parts)
    part = x_parts[0].shape[0]
    return pl.pallas_call(
        lambda *refs: acts_kernel(
            turn, slots, stride, routes.shape[0], offsets, len(panel), *refs
        ),
        out_shape=jax.ShapeDtypeStruct((3 * panel[0].shape[-2], parts * part), BF16),
        in_specs=[whole_in_vmem()] * (2 * parts + len(panel) + 2) + [untouched()] * len(after),
        out_specs=whole_in_vmem(),
        compiler_params=pltpu.CompilerParams(vmem_limit_bytes=VMEM_LIMIT),
        cost_estimate=NO_COST,
        name=f"acts_{turn}_{name}",
    )(*x_parts, *dy_parts, *panel, routes, weight, *after)


def grads_kernel(parts, groups, kinds, *refs):
    x_refs, dy_refs = refs[:parts], refs[parts : 2 * parts]
    acts, grads = refs[2 * parts : 2 * parts + groups], refs[-kinds:]
    if kinds == 1:
        grads = [grads[0].at[kind] for kind in range(3)]
    units, width = grads[0].shape
    columns = tile_of(width, 512)
    for start in range(0, width, columns):
        here = slice(start, start + columns)
        x = jnp.concatenate([ref[:, here] for ref in x_refs], axis=0)
        dy = jnp.concatenate([ref[:, here] for ref in dy_refs], axis=0)
        d_both = jnp.concatenate([act[0 : 2 * units, :] for act in acts], axis=1)
        d_both = jnp.dot(d_both, x, preferred_element_type=F32).astype(BF16)
        grads[0][:, here] = d_both[0:units]
        grads[1][:, here] = d_both[units:]
        hidden = jnp.concatenate([act[2 * units : 3 * units, :] for act in acts], axis=1)
        grads[2][:, here] = jnp.dot(hidden, dy, preferred_element_type=F32).astype(BF16)


def grads_pass(turn, x_parts, dy_parts, acts, shapes, after=()):
    parts = len(x_parts)
    return pl.pallas_call(
        lambda *refs: grads_kernel(parts, len(acts), len(shapes), *refs),
        out_shape=tuple(jax.ShapeDtypeStruct(shape, BF16) for shape in shapes),
        in_specs=[whole_in_vmem()] * (2 * parts + len(acts)) + [untouched()] * len(after),
        out_specs=tuple(whole_in_vmem() for _ in shapes),
        compiler_params=pltpu.CompilerParams(vmem_limit_bytes=VMEM_LIMIT),
        cost_estimate=work_cost(6 * parts * acts[0].shape[0] // 3 * x_parts[0].size),
        name=f"grads_{turn}",
    )(*x_parts, *dy_parts, *acts, *after)


def chunk_kernel(wanted, slots, part, acts, panels, outs):
    units, width = panels[0][0].shape
    columns = tile_of(width, 512)

    @pl.loop(0, width // columns)
    def _(step):
        here = pl.ds(pl.multiple_of(step * columns, columns), columns)
        kinds = {"mixed": (2, 3), "grad": (0, 2)}
        sides = {
            kind: jnp.concatenate(
                [panel[which][:, here] for panel in panels for which in range(*span)], axis=0
            )
            for kind, span in kinds.items()
        }
        for out, (kind, group, row) in zip(outs, wanted):
            low, high = (units * which for which in kinds[kind])
            act = jnp.concatenate(
                [act[group][low:high, row * part : (row + 1) * part] for act in acts], axis=0
            )
            total = lax.dot_general(act, sides[kind], CONTRACT_FIRST, preferred_element_type=F32)
            out[:, here] = total.astype(BF16)


def chunk_pass(wanted, acts, panels, groups, part, cost, after=()):
    slots = len(panels)
    width = panels[0][0].shape[-1]
    pieces = [len(panel) for panel in panels]
    named = [
        (kind, g, group.index(d)) for kind, d in wanted for g, group in enumerate(groups) if d in group
    ]

    def kernel(*refs):
        act_refs = [refs[s * len(groups) : (s + 1) * len(groups)] for s in range(slots)]
        rest = refs[slots * len(groups) :]
        starts = [sum(pieces[:s]) for s in range(slots)]
        panel_refs = [by_kind(rest[a : a + n]) for a, n in zip(starts, pieces)]
        chunk_kernel(named, slots, part, act_refs, panel_refs, rest[sum(pieces) + len(after) :])

    return pl.pallas_call(
        kernel,
        out_shape=tuple(jax.ShapeDtypeStruct((part, width), BF16) for _ in wanted),
        in_specs=[whole_in_vmem()] * (slots * len(groups) + sum(pieces)) + [untouched()] * len(after),
        out_specs=tuple(whole_in_vmem() for _ in wanted),
        compiler_params=pltpu.CompilerParams(vmem_limit_bytes=VMEM_LIMIT),
        cost_estimate=cost,
        name=f"chunks_{len(wanted)}",
    )(*[act for slot_acts in acts for act in slot_acts], *[piece for panel in panels for piece in panel], *after)


def final_rows_kernel(*refs):
    a, b, out, token = refs[0], refs[1], *refs[-2:]
    out[...] = (a[...].astype(F32) + b[...]).astype(out.dtype)
    token[...] = jnp.zeros_like(token)


def final_rows(a, b, cost, after):
    return pl.pallas_call(
        final_rows_kernel,
        out_shape=(jax.ShapeDtypeStruct(a.shape, BF16), token_shape()),
        in_specs=[whole_in_vmem()] * 2 + [untouched()] * len(after),
        out_specs=(whole_in_vmem(), whole_in_vmem()),
        compiler_params=pltpu.CompilerParams(vmem_limit_bytes=VMEM_LIMIT),
        cost_estimate=cost,
        name="final_rows",
    )(a, b, *after)


class Line:
    def __init__(self):
        self.tail = ()

    def step(self, make):
        out = make(self.tail)
        self.tail = (out[-1] if isinstance(out, (tuple, list)) else out,)
        return out

    def arrive(self, value):
        return self.step(lambda after: gate(value, after))


def body(tokens, cotangent, routes, route_weight, fetch_pick, panels):
    panels = pltpu.with_memory_space_constraint(panels, pltpu.HBM)
    fetch_pick = pltpu.with_memory_space_constraint(fetch_pick, pltpu.HBM)
    slots = fetch_pick.shape[1]
    stride = lax.axis_size("node") // slots
    part, width = tokens.shape
    order = ring_order(lax.axis_size("local"))
    size = len(order)
    up_most, down_most = size // 2, size - 1 - size // 2
    last, late = slots - 1, slots - 2
    middle = list(range(1, late))
    line = Line()

    ring_routes = routes.reshape(size, part)
    ring_weight = route_weight.reshape(size, part)
    near = [d for d in range(size) if min(d, size - d) <= size // 4 and d != size // 4]
    groups = [near, [d for d in range(size) if d not in near]]
    rows = [d for group in groups for d in group]
    x_parts = [tokens] + [None] * (size - 1)
    dy_parts = [cotangent] + [None] * (size - 1)
    acts = [[None, None] for _ in range(slots)]
    grads, back = [None] * slots, [None] * slots

    def make_acts(turn, g):
        take = groups[g]
        acts[turn][g] = line.step(
            lambda after: acts_pass(
                "nf"[g],
                turn,
                slots,
                stride,
                take,
                [x_parts[d] for d in take],
                [dy_parts[d] for d in take],
                read[turn],
                ring_routes,
                ring_weight,
                after,
            )
        )

    def make_grads(turn):
        shape = panels.shape[1:]
        grads[turn] = line.step(
            lambda after: grads_pass(
                turn,
                [x_parts[d] for d in rows],
                [dy_parts[d] for d in rows],
                acts[turn],
                [shape[1:]] * shape[0] if turn in middle else [shape],
                after,
            )
        )
        if turn != last:
            back[turn] = [exchange(grad, turn, slots) if turn else grad for grad in grads[turn]]

    read = [None] * slots
    picked = line.step(lambda after: pick_pass([late], stride, fetch_pick, panels, False, after))
    read[late] = [exchange(picked[0], late, slots)]
    for turn in middle:
        picked = line.step(lambda after: pick_pass([turn], stride, fetch_pick, panels, True, after))
        read[turn] = [exchange(piece, turn, slots) for piece in picked]
    picked = line.step(lambda after: pick_pass([last, 0], stride, fetch_pick, panels, False, after))
    read[last], read[0] = [[piece] for piece in picked]

    chains = [(x_parts, 1, up_most), (dy_parts, -1, up_most), (x_parts, -1, down_most), (dy_parts, 1, down_most)]
    moving = [ring_step(parts[0], order, way) for parts, way, _ in chains]
    for turn in middle:
        read[turn] = [line.arrive(piece) for piece in read[turn]]
    for hop in range(1, up_most + 1):
        for i, (parts, way, hops) in enumerate(chains):
            if hop > hops:
                continue
            if hop == max(1, up_most // 2) and i == 2:
                read[late] = [line.arrive(read[late][0])]
                read[last] = [exchange(line.arrive(read[last][0]), last, slots)]
            arrived = line.arrive(moving[i])
            parts[-way * hop % size] = arrived
            if hop < hops:
                moving[i] = ring_step(arrived, order, way)
            if hop == max(1, up_most // 2) and i == len(chains) - 1:
                for turn in middle + [0, late]:
                    make_acts(turn, 0)

    make_acts(late, 1)
    make_grads(late)
    for turn in middle:
        make_acts(turn, 1)
        make_grads(turn)
    make_acts(0, 1)
    read[last] = [line.arrive(read[last][0])]
    make_acts(last, 1)
    make_acts(last, 0)
    for turn in middle:
        back[turn] = [line.arrive(grad) for grad in back[turn]]

    kinds = ("mixed", "grad")
    early = [("mixed", up_most), ("grad", size - up_most), ("mixed", size - down_most), ("grad", down_most)]
    early_cost = work_cost(6 * len(early) * slots * part * read[0][0].size // 6)
    later = [(kind, d) for kind in kinds for d in range(size) if (kind, d) not in early]
    chunks = dict(zip(early, line.step(lambda after: chunk_pass(early, acts, read, groups, part, early_cost, after))))
    chains = [("mixed", 1, up_most), ("grad", -1, up_most), ("mixed", -1, down_most), ("grad", 1, down_most)]
    moving = [ring_step(chunks[kind, way * hops % size], order, way) for kind, way, hops in chains]
    chunks.update(zip(later, line.step(lambda after: chunk_pass(later, acts, read, groups, part, NO_COST, after))))
    make_grads(last)
    make_grads(0)

    sums = {}
    for hop in range(1, up_most + 1):
        for i, (kind, way, hops) in enumerate(chains):
            if hop > hops:
                continue
            if hop == max(1, up_most // 2) and i == 2:
                back[late] = [line.arrive(back[late][0])]
                back[last] = exchange(line.arrive(grads[last][0]), last, slots)
            left = hops - hop
            if left:
                chunk = chunks[kind, way * left % size]
                arrived = line.step(lambda after: add_rows(moving[i], chunk, BF16, after))
                moving[i] = ring_step(arrived, order, way)
            elif kind not in sums:
                sums[kind] = line.step(lambda after: add_rows(moving[i], chunks[kind, 0], F32, after))
                if len(sums) == 2:
                    panel_grad, base, _ = line.step(
                        lambda after: total_pass(
                            list(range(last)), last, stride, fetch_pick, back[:last], panels.shape, after
                        )
                    )
            else:
                cost = work_cost(LAST_FLOPS) if (kind, hop) == (chains[1][0], up_most) else NO_COST
                sums[kind], _ = line.step(lambda after: final_rows(moving[i], sums[kind], cost, after))
    back[last] = line.arrive(back[last])
    panel_grad = add_pass(last, stride, fetch_pick, panel_grad, base, back[last])
    return sums["mixed"], sums["grad"], panel_grad


def solution(mesh):
    return jax.shard_map(
        body,
        mesh=mesh,
        in_specs=(
            P(("node", "local"), None),
            P(("node", "local"), None),
            P("node", None),
            P("node", None),
            P(),
            P("node", None, "local", None),
        ),
        out_specs=(
            P(("node", "local"), None),
            P(("node", "local"), None),
            P("node", None, "local", None),
        ),
        check_vma=False,
    )
```

```python
import jax
import jax.numpy as jnp
from jax import lax
from jax.experimental import pallas as pl
from jax.experimental.pallas import tpu as pltpu
from jax.sharding import PartitionSpec as P

BF16 = jnp.bfloat16
F32 = jnp.float32
VMEM_LIMIT = 24 * 1024 * 1024
NO_COST = pl.CostEstimate(flops=1, bytes_accessed=1, transcendentals=0)


LAST_FLOPS = 12 * 10**9


def work_cost(flops):
    return pl.CostEstimate(flops=flops, bytes_accessed=1, transcendentals=0)


CONTRACT_LAST = (((1,), (1,)), ((), ()))
CONTRACT_FIRST = (((0,), (0,)), ((), ()))


def whole_in_vmem():
    return pl.BlockSpec(memory_space=pltpu.VMEM)


def in_hbm():
    return pl.BlockSpec(memory_space=pltpu.HBM)


def token_shape():
    return jax.ShapeDtypeStruct((8, 128), F32)


def by_kind(refs):
    return [refs[0].at[kind] for kind in range(3)] if len(refs) == 1 else list(refs)


def untouched():
    return pl.BlockSpec(memory_space=pl.ANY)


def tile_of(size, most):
    tile = min(size, most)
    while size % tile:
        tile -= 1
    return tile


def ring_order(size):
    return list(range(0, size, 2)) + list(range(1, size, 2))[::-1]


def ring_source(size, ahead):
    me = lax.axis_index("local")
    half = lax.div(size + 1, 2)
    place = jnp.where(lax.rem(me, 2) == 0, lax.div(me, 2), size - 1 - lax.div(me, 2))
    there = lax.rem(place + ahead, size)
    return jnp.where(there < half, 2 * there, 2 * (size - 1 - there) + 1)


def partner_of(place, turn, slots):
    return place ^ turn


def owner_of(node, turn, slots, stride):
    return partner_of(node // stride, turn, slots) * stride + node % stride


def turn_slot(turn, slots, stride):
    place = lax.div(lax.axis_index("node"), stride)
    return lax.rem(place - partner_of(place, turn, slots) + slots, slots)


def turn_pick(fetch_pick, turn, stride):
    slots = fetch_pick.shape[1]
    node = lax.axis_index("node")
    place = lax.div(node, stride)
    partner = partner_of(place, turn, slots)
    reader = partner * stride + lax.rem(node, stride)
    return fetch_pick[reader, lax.rem(partner - place + slots, slots)]


def exchange(block, turn, slots):
    size = lax.axis_size("node")
    stride = size // slots
    return lax.ppermute(
        block, "node", [(owner_of(node, turn, slots, stride), node) for node in range(size)]
    )


def halves(units):
    middle = max(16, units // 32 * 16) if units > 16 else units
    return [(0, middle), (middle, units)] if middle < units else [(0, units)]


def pick_kernel(turns, stride, apart, fetch_pick, panels, *refs):
    kinds, units = panels.shape[1:3]
    spans = halves(units)
    outs, sems = refs[-len(turns) * (kinds if apart else 1) - 1 : -1], refs[-1]
    copies = []
    for i, turn in enumerate(turns):
        pick = turn_pick(fetch_pick, turn, stride)
        for kind in range(kinds):
            out = outs[i * kinds + kind] if apart else outs[i].at[kind]
            for j, (low, high) in enumerate(spans):
                here = pl.ds(low, high - low)
                copies.append(
                    pltpu.make_async_copy(
                        panels.at[pick, kind, here], out.at[here], sems.at[i, kind, j]
                    )
                )
    for copy in copies:
        copy.start()
    for copy in copies:
        copy.wait()


def pick_pass(turns, stride, fetch_pick, panels, apart, after=()):
    kinds = panels.shape[1]
    shapes = [panels.shape[2:]] * kinds if apart else [panels.shape[1:]]
    shapes = shapes * len(turns)
    out = pl.pallas_call(
        lambda *refs: pick_kernel(turns, stride, apart, *refs),
        out_shape=tuple(jax.ShapeDtypeStruct(shape, BF16) for shape in shapes),
        in_specs=[pl.BlockSpec(memory_space=pltpu.SMEM), in_hbm()] + [untouched()] * len(after),
        out_specs=tuple(untouched() for _ in shapes),
        scratch_shapes=[pltpu.SemaphoreType.DMA((len(turns), kinds, 2))],
        compiler_params=pltpu.CompilerParams(vmem_limit_bytes=1024 * 1024),
        cost_estimate=NO_COST,
        name="pick",
    )(fetch_pick, panels, *after)
    return out


def gate(value, after):
    return pl.pallas_call(
        lambda *refs: None,
        out_shape=jax.ShapeDtypeStruct(value.shape, value.dtype),
        in_specs=[untouched()] * (1 + len(after)),
        out_specs=untouched(),
        input_output_aliases={0: 0},
        compiler_params=pltpu.CompilerParams(vmem_limit_bytes=1024 * 1024),
        cost_estimate=NO_COST,
        name="gate",
    )(value, *after)


def total_kernel(turns, last, stride, counts, fetch_pick, *refs):
    out, base, token, refs = *refs[-3:], list(refs[: sum(counts)])
    picks = [turn_pick(fetch_pick, turn, stride) for turn in turns]
    last_pick = turn_pick(fetch_pick, last, stride)
    token[...] = jnp.zeros_like(token)
    experts, kinds = out.shape[:2]
    grads = []
    for count in counts:
        taken, refs = refs[:count], refs[count:]
        grads.append([taken[0].at[kind] for kind in range(kinds)] if count == 1 else taken)
    for kind in range(kinds):
        terms = [grad[kind][...].astype(F32) for grad in grads]
        for e in range(experts):
            total = jnp.zeros(terms[0].shape, F32)
            for pick, term in zip(picks, terms):
                total += jnp.where(pick == e, term, 0.0)
            total = total.astype(BF16)
            out[e, kind] = total
            if e == 0:
                base[kind] = total
            else:

                @pl.when(last_pick == e)
                def _():
                    base[kind] = total


def total_pass(turns, last, stride, fetch_pick, grads, shape, after):
    counts = [len(grad) for grad in grads]
    return pl.pallas_call(
        lambda *refs: total_kernel(turns, last, stride, counts, *refs),
        out_shape=(
            jax.ShapeDtypeStruct(shape, BF16),
            jax.ShapeDtypeStruct(shape[1:], BF16),
            token_shape(),
        ),
        in_specs=[pl.BlockSpec(memory_space=pltpu.SMEM)]
        + [whole_in_vmem()] * sum(counts)
        + [untouched()] * len(after),
        out_specs=(whole_in_vmem(),) * 3,
        compiler_params=pltpu.CompilerParams(vmem_limit_bytes=VMEM_LIMIT),
        cost_estimate=NO_COST,
        name="total",
    )(fetch_pick, *[grad for slot_grads in grads for grad in slot_grads], *after)


def add_kernel(turn, stride, fetch_pick, total, base, grad, out, sums, sems):
    pick = turn_pick(fetch_pick, turn, stride)
    writes = []
    for kind in range(grad.shape[0]):
        for j, (low, high) in enumerate(halves(grad.shape[1])):
            here = pl.ds(low, high - low)
            sums[kind, here] = (base[kind, here].astype(F32) + grad[kind, here].astype(F32)).astype(BF16)
            write = pltpu.make_async_copy(
                sums.at[kind, here], out.at[pick, kind, here], sems.at[kind, j]
            )
            write.start()
            writes.append(write)
    for write in writes:
        write.wait()


def add_pass(turn, stride, fetch_pick, total, base, grad):
    return pl.pallas_call(
        lambda *refs: add_kernel(turn, stride, *refs),
        out_shape=jax.ShapeDtypeStruct(total.shape, BF16),
        in_specs=[pl.BlockSpec(memory_space=pltpu.SMEM), in_hbm(), whole_in_vmem(), whole_in_vmem()],
        out_specs=in_hbm(),
        input_output_aliases={1: 0},
        scratch_shapes=[pltpu.VMEM(grad.shape, BF16), pltpu.SemaphoreType.DMA((grad.shape[0], 2))],
        compiler_params=pltpu.CompilerParams(vmem_limit_bytes=12 * 1024 * 1024),
        cost_estimate=NO_COST,
        name="add",
    )(fetch_pick, total, base, grad)


def ring_step(block, order, distance):
    size = len(order)
    return lax.ppermute(
        block, "local", [(order[i], order[(i + distance) % size]) for i in range(size)]
    )


def add_rows_kernel(*refs):
    a, b, out = refs[0], refs[1], refs[-1]
    out[...] = (a[...].astype(F32) + b[...].astype(F32)).astype(out.dtype)


def add_rows(a, b, dtype, after=()):
    return pl.pallas_call(
        add_rows_kernel,
        out_shape=jax.ShapeDtypeStruct(a.shape, dtype),
        in_specs=[whole_in_vmem()] * 2 + [untouched()] * len(after),
        out_specs=whole_in_vmem(),
        compiler_params=pltpu.CompilerParams(vmem_limit_bytes=VMEM_LIMIT),
        cost_estimate=NO_COST,
        name="add_rows",
    )(a, b, *after)


def acts_kernel(turn, slots, stride, size, offsets, pieces, *refs):
    parts = len(offsets)
    x_refs, dy_refs = refs[:parts], refs[parts : 2 * parts]
    panel, (routes, weight), acts = by_kind(refs[2 * parts : 2 * parts + pieces]), refs[
        2 * parts + pieces : 2 * parts + pieces + 2
    ], refs[-1]
    units, width = panel[0].shape
    part = x_refs[0].shape[0]
    at_once = 2 if parts % 2 == 0 else 1
    slot = turn_slot(turn, slots, stride)
    for d in range(0, parts, at_once):
        here = slice(d * part, (d + at_once) * part)
        x = jnp.concatenate([ref[...] for ref in x_refs[d : d + at_once]], axis=0)
        dy = jnp.concatenate([ref[...] for ref in dy_refs[d : d + at_once]], axis=0)
        both = lax.dot_general(
            jnp.concatenate([panel[0][...], panel[1][...]], axis=0), x, CONTRACT_LAST, preferred_element_type=F32
        )
        gate, up = both[:units], both[units:]
        d_hidden = lax.dot_general(panel[2][...], dy, CONTRACT_LAST, preferred_element_type=F32)
        sources = [ring_source(size, ahead) for ahead in offsets[d : d + at_once]]
        scale = jnp.concatenate(
            [
                jnp.where(routes[pl.ds(i, 1), :] == slot, weight[pl.ds(i, 1), :], 0.0)
                for i in sources
            ],
            axis=1,
        )
        sigmoid_gate = jax.nn.sigmoid(gate)
        activated = gate * sigmoid_gate
        d_hidden = d_hidden * scale
        d_gate = d_hidden * up * sigmoid_gate * (1.0 + gate * (1.0 - sigmoid_gate))
        acts[0:units, here] = d_gate.astype(BF16)
        acts[units : 2 * units, here] = (d_hidden * activated).astype(BF16)
        acts[2 * units : 3 * units, here] = (activated * up * scale).astype(BF16)


def acts_pass(name, turn, slots, stride, offsets, x_parts, dy_parts, panel, routes, weight, after=()):
    parts = len(x_parts)
    part = x_parts[0].shape[0]
    return pl.pallas_call(
        lambda *refs: acts_kernel(
            turn, slots, stride, routes.shape[0], offsets, len(panel), *refs
        ),
        out_shape=jax.ShapeDtypeStruct((3 * panel[0].shape[-2], parts * part), BF16),
        in_specs=[whole_in_vmem()] * (2 * parts + len(panel) + 2) + [untouched()] * len(after),
        out_specs=whole_in_vmem(),
        compiler_params=pltpu.CompilerParams(vmem_limit_bytes=VMEM_LIMIT),
        cost_estimate=NO_COST,
        name=f"acts_{turn}_{name}",
    )(*x_parts, *dy_parts, *panel, routes, weight, *after)


def grads_kernel(parts, groups, kinds, *refs):
    x_refs, dy_refs = refs[:parts], refs[parts : 2 * parts]
    acts, grads = refs[2 * parts : 2 * parts + groups], refs[-kinds:]
    if kinds == 1:
        grads = [grads[0].at[kind] for kind in range(3)]
    units, width = grads[0].shape
    columns = tile_of(width, 512)
    for start in range(0, width, columns):
        here = slice(start, start + columns)
        x = jnp.concatenate([ref[:, here] for ref in x_refs], axis=0)
        dy = jnp.concatenate([ref[:, here] for ref in dy_refs], axis=0)
        d_both = jnp.concatenate([act[0 : 2 * units, :] for act in acts], axis=1)
        d_both = jnp.dot(d_both, x, preferred_element_type=F32).astype(BF16)
        grads[0][:, here] = d_both[0:units]
        grads[1][:, here] = d_both[units:]
        hidden = jnp.concatenate([act[2 * units : 3 * units, :] for act in acts], axis=1)
        grads[2][:, here] = jnp.dot(hidden, dy, preferred_element_type=F32).astype(BF16)


def grads_pass(turn, x_parts, dy_parts, acts, shapes, after=()):
    parts = len(x_parts)
    return pl.pallas_call(
        lambda *refs: grads_kernel(parts, len(acts), len(shapes), *refs),
        out_shape=tuple(jax.ShapeDtypeStruct(shape, BF16) for shape in shapes),
        in_specs=[whole_in_vmem()] * (2 * parts + len(acts)) + [untouched()] * len(after),
        out_specs=tuple(whole_in_vmem() for _ in shapes),
        compiler_params=pltpu.CompilerParams(vmem_limit_bytes=VMEM_LIMIT),
        cost_estimate=work_cost(6 * parts * acts[0].shape[0] // 3 * x_parts[0].size),
        name=f"grads_{turn}",
    )(*x_parts, *dy_parts, *acts, *after)


def chunk_kernel(wanted, slots, part, acts, panels, outs):
    units, width = panels[0][0].shape
    columns = tile_of(width, 512)

    @pl.loop(0, width // columns)
    def _(step):
        here = pl.ds(pl.multiple_of(step * columns, columns), columns)
        kinds = {"mixed": (2, 3), "grad": (0, 2)}
        sides = {
            kind: jnp.concatenate(
                [panel[which][:, here] for panel in panels for which in range(*span)], axis=0
            )
            for kind, span in kinds.items()
        }
        for out, (kind, group, row) in zip(outs, wanted):
            low, high = (units * which for which in kinds[kind])
            act = jnp.concatenate(
                [act[group][low:high, row * part : (row + 1) * part] for act in acts], axis=0
            )
            total = lax.dot_general(act, sides[kind], CONTRACT_FIRST, preferred_element_type=F32)
            out[:, here] = total.astype(BF16)


def chunk_pass(wanted, acts, panels, groups, part, cost, after=()):
    slots = len(panels)
    width = panels[0][0].shape[-1]
    pieces = [len(panel) for panel in panels]
    named = [
        (kind, g, group.index(d)) for kind, d in wanted for g, group in enumerate(groups) if d in group
    ]

    def kernel(*refs):
        act_refs = [refs[s * len(groups) : (s + 1) * len(groups)] for s in range(slots)]
        rest = refs[slots * len(groups) :]
        starts = [sum(pieces[:s]) for s in range(slots)]
        panel_refs = [by_kind(rest[a : a + n]) for a, n in zip(starts, pieces)]
        chunk_kernel(named, slots, part, act_refs, panel_refs, rest[sum(pieces) + len(after) :])

    return pl.pallas_call(
        kernel,
        out_shape=tuple(jax.ShapeDtypeStruct((part, width), BF16) for _ in wanted),
        in_specs=[whole_in_vmem()] * (slots * len(groups) + sum(pieces)) + [untouched()] * len(after),
        out_specs=tuple(whole_in_vmem() for _ in wanted),
        compiler_params=pltpu.CompilerParams(vmem_limit_bytes=VMEM_LIMIT),
        cost_estimate=cost,
        name=f"chunks_{len(wanted)}",
    )(*[act for slot_acts in acts for act in slot_acts], *[piece for panel in panels for piece in panel], *after)


def final_rows_kernel(*refs):
    a, b, out, token = refs[0], refs[1], *refs[-2:]
    out[...] = (a[...].astype(F32) + b[...]).astype(out.dtype)
    token[...] = jnp.zeros_like(token)


def final_rows(a, b, cost, after):
    return pl.pallas_call(
        final_rows_kernel,
        out_shape=(jax.ShapeDtypeStruct(a.shape, BF16), token_shape()),
        in_specs=[whole_in_vmem()] * 2 + [untouched()] * len(after),
        out_specs=(whole_in_vmem(), whole_in_vmem()),
        compiler_params=pltpu.CompilerParams(vmem_limit_bytes=VMEM_LIMIT),
        cost_estimate=cost,
        name="final_rows",
    )(a, b, *after)


class Line:
    def __init__(self):
        self.tail = ()

    def step(self, make):
        out = make(self.tail)
        self.tail = (out[-1] if isinstance(out, (tuple, list)) else out,)
        return out

    def arrive(self, value):
        return self.step(lambda after: gate(value, after))


def body(tokens, cotangent, routes, route_weight, fetch_pick, panels):
    panels = pltpu.with_memory_space_constraint(panels, pltpu.HBM)
    fetch_pick_far = pltpu.with_memory_space_constraint(fetch_pick, pltpu.HBM)
    slots = fetch_pick.shape[1]
    stride = lax.axis_size("node") // slots
    part, width = tokens.shape
    order = ring_order(lax.axis_size("local"))
    size = len(order)
    up_most, down_most = size // 2, size - 1 - size // 2
    last, late = slots - 1, slots - 2
    middle = list(range(1, late))
    line = Line()

    ring_routes = routes.reshape(size, part)
    ring_weight = route_weight.reshape(size, part)
    near = [d for d in range(size) if min(d, size - d) <= size // 4 and d != size // 4]
    groups = [near, [d for d in range(size) if d not in near]]
    rows = [d for group in groups for d in group]
    x_parts = [tokens] + [None] * (size - 1)
    dy_parts = [cotangent] + [None] * (size - 1)
    acts = [[None, None] for _ in range(slots)]
    grads, back = [None] * slots, [None] * slots

    def make_acts(turn, g):
        take = groups[g]
        acts[turn][g] = line.step(
            lambda after: acts_pass(
                "nf"[g],
                turn,
                slots,
                stride,
                take,
                [x_parts[d] for d in take],
                [dy_parts[d] for d in take],
                read[turn],
                ring_routes,
                ring_weight,
                after,
            )
        )

    def make_grads(turn):
        shape = panels.shape[1:]
        grads[turn] = line.step(
            lambda after: grads_pass(
                turn,
                [x_parts[d] for d in rows],
                [dy_parts[d] for d in rows],
                acts[turn],
                [shape[1:]] * shape[0] if turn in middle else [shape],
                after,
            )
        )
        if turn != last:
            back[turn] = [exchange(grad, turn, slots) if turn else grad for grad in grads[turn]]

    read = [None] * slots
    picked = line.step(lambda after: pick_pass([late], stride, fetch_pick_far, panels, False, after))
    read[late] = [exchange(picked[0], late, slots)]
    for turn in middle:
        picked = line.step(lambda after: pick_pass([turn], stride, fetch_pick, panels, True, after))
        read[turn] = [exchange(piece, turn, slots) for piece in picked]
    picked = line.step(lambda after: pick_pass([last, 0], stride, fetch_pick, panels, False, after))
    read[last], read[0] = [[piece] for piece in picked]

    chains = [(x_parts, 1, up_most), (dy_parts, -1, up_most), (x_parts, -1, down_most), (dy_parts, 1, down_most)]
    moving = [ring_step(parts[0], order, way) for parts, way, _ in chains]
    for turn in middle:
        read[turn] = [line.arrive(piece) for piece in read[turn]]
    for hop in range(1, up_most + 1):
        for i, (parts, way, hops) in enumerate(chains):
            if hop > hops:
                continue
            if hop == max(1, up_most // 2) and i == 2:
                read[late] = [line.arrive(read[late][0])]
                read[last] = [exchange(line.arrive(read[last][0]), last, slots)]
            arrived = line.arrive(moving[i])
            parts[-way * hop % size] = arrived
            if hop < hops:
                moving[i] = ring_step(arrived, order, way)
            if hop == max(1, up_most // 2) and i == len(chains) - 1:
                for turn in middle + [0, late]:
                    make_acts(turn, 0)

    make_acts(late, 1)
    make_grads(late)
    for turn in middle:
        make_acts(turn, 1)
        make_grads(turn)
    make_acts(0, 1)
    read[last] = [line.arrive(read[last][0])]
    make_acts(last, 1)
    make_acts(last, 0)
    for turn in middle:
        back[turn] = [line.arrive(grad) for grad in back[turn]]

    kinds = ("mixed", "grad")
    early = [("mixed", up_most), ("grad", size - up_most), ("mixed", size - down_most), ("grad", down_most)]
    early_cost = work_cost(6 * len(early) * slots * part * read[0][0].size // 6)
    later = [(kind, d) for kind in kinds for d in range(size) if (kind, d) not in early]
    chunks = dict(zip(early, line.step(lambda after: chunk_pass(early, acts, read, groups, part, early_cost, after))))
    chains = [("mixed", 1, up_most), ("grad", -1, up_most), ("mixed", -1, down_most), ("grad", 1, down_most)]
    moving = [ring_step(chunks[kind, way * hops % size], order, way) for kind, way, hops in chains]
    chunks.update(zip(later, line.step(lambda after: chunk_pass(later, acts, read, groups, part, NO_COST, after))))
    make_grads(last)
    make_grads(0)

    sums = {}
    for hop in range(1, up_most + 1):
        for i, (kind, way, hops) in enumerate(chains):
            if hop > hops:
                continue
            if hop == max(1, up_most // 2) and i == 2:
                back[late] = [line.arrive(back[late][0])]
                back[last] = exchange(line.arrive(grads[last][0]), last, slots)
            left = hops - hop
            if left:
                chunk = chunks[kind, way * left % size]
                arrived = line.step(lambda after: add_rows(moving[i], chunk, BF16, after))
                moving[i] = ring_step(arrived, order, way)
            elif kind not in sums:
                sums[kind] = line.step(lambda after: add_rows(moving[i], chunks[kind, 0], F32, after))
                if len(sums) == 2:
                    panel_grad, base, _ = line.step(
                        lambda after: total_pass(
                            list(range(last)), last, stride, fetch_pick, back[:last], panels.shape, after
                        )
                    )
            else:
                cost = work_cost(LAST_FLOPS) if (kind, hop) == (chains[1][0], up_most) else NO_COST
                sums[kind], _ = line.step(lambda after: final_rows(moving[i], sums[kind], cost, after))
    back[last] = line.arrive(back[last])
    panel_grad = add_pass(last, stride, fetch_pick, panel_grad, base, back[last])
    return sums["mixed"], sums["grad"], panel_grad


def solution(mesh):
    return jax.shard_map(
        body,
        mesh=mesh,
        in_specs=(
            P(("node", "local"), None),
            P(("node", "local"), None),
            P("node", None),
            P("node", None),
            P(),
            P("node", None, "local", None),
        ),
        out_specs=(
            P(("node", "local"), None),
            P(("node", "local"), None),
            P("node", None, "local", None),
        ),
        check_vma=False,
    )
```

```python
import jax
import jax.numpy as jnp
from jax import lax
from jax.experimental import pallas as pl
from jax.experimental.pallas import tpu as pltpu
from jax.sharding import PartitionSpec as P

BF16 = jnp.bfloat16
F32 = jnp.float32
VMEM_LIMIT = 24 * 1024 * 1024
NO_COST = pl.CostEstimate(flops=1, bytes_accessed=1, transcendentals=0)


LAST_FLOPS = 12 * 10**9


def work_cost(flops):
    return pl.CostEstimate(flops=flops, bytes_accessed=1, transcendentals=0)


CONTRACT_LAST = (((1,), (1,)), ((), ()))
CONTRACT_FIRST = (((0,), (0,)), ((), ()))


def whole_in_vmem():
    return pl.BlockSpec(memory_space=pltpu.VMEM)


def in_hbm():
    return pl.BlockSpec(memory_space=pltpu.HBM)


def token_shape():
    return jax.ShapeDtypeStruct((8, 128), F32)


def by_kind(refs):
    return [refs[0].at[kind] for kind in range(3)] if len(refs) == 1 else list(refs)


def untouched():
    return pl.BlockSpec(memory_space=pl.ANY)


def tile_of(size, most):
    tile = min(size, most)
    while size % tile:
        tile -= 1
    return tile


def ring_order(size):
    return list(range(0, size, 2)) + list(range(1, size, 2))[::-1]


def ring_source(size, ahead):
    me = lax.axis_index("local")
    half = lax.div(size + 1, 2)
    place = jnp.where(lax.rem(me, 2) == 0, lax.div(me, 2), size - 1 - lax.div(me, 2))
    there = lax.rem(place + ahead, size)
    return jnp.where(there < half, 2 * there, 2 * (size - 1 - there) + 1)


def partner_of(place, turn, slots):
    return place ^ turn


def owner_of(node, turn, slots, stride):
    return partner_of(node // stride, turn, slots) * stride + node % stride


def turn_slot(turn, slots, stride):
    place = lax.div(lax.axis_index("node"), stride)
    return lax.rem(place - partner_of(place, turn, slots) + slots, slots)


def turn_pick(fetch_pick, turn, stride):
    slots = fetch_pick.shape[1]
    node = lax.axis_index("node")
    place = lax.div(node, stride)
    partner = partner_of(place, turn, slots)
    reader = partner * stride + lax.rem(node, stride)
    return fetch_pick[reader, lax.rem(partner - place + slots, slots)]


def exchange(block, turn, slots):
    size = lax.axis_size("node")
    stride = size // slots
    return lax.ppermute(
        block, "node", [(owner_of(node, turn, slots, stride), node) for node in range(size)]
    )


def spans_of(units, most=4):
    tiles = max(1, units // 16)
    count = min(most, tiles)
    cuts = [tiles * i // count * 16 for i in range(count)] + [units]
    return list(zip(cuts[:-1], cuts[1:]))


def pick_kernel(turns, stride, apart, fetch_pick, panels, *refs):
    kinds, units = panels.shape[1:3]
    spans = spans_of(units)
    outs, sems = refs[-len(turns) * (kinds if apart else 1) - 1 : -1], refs[-1]
    copies = []
    for i, turn in enumerate(turns):
        pick = turn_pick(fetch_pick, turn, stride)
        for kind in range(kinds):
            out = outs[i * kinds + kind] if apart else outs[i].at[kind]
            for j, (low, high) in enumerate(spans):
                here = pl.ds(low, high - low)
                copies.append(
                    pltpu.make_async_copy(
                        panels.at[pick, kind, here], out.at[here], sems.at[i, kind, j]
                    )
                )
    for copy in copies:
        copy.start()
    for copy in copies:
        copy.wait()


def pick_pass(turns, stride, fetch_pick, panels, apart, after=()):
    kinds = panels.shape[1]
    shapes = [panels.shape[2:]] * kinds if apart else [panels.shape[1:]]
    shapes = shapes * len(turns)
    out = pl.pallas_call(
        lambda *refs: pick_kernel(turns, stride, apart, *refs),
        out_shape=tuple(jax.ShapeDtypeStruct(shape, BF16) for shape in shapes),
        in_specs=[pl.BlockSpec(memory_space=pltpu.SMEM), in_hbm()] + [untouched()] * len(after),
        out_specs=tuple(untouched() for _ in shapes),
        scratch_shapes=[pltpu.SemaphoreType.DMA((len(turns), kinds, 4))],
        compiler_params=pltpu.CompilerParams(vmem_limit_bytes=1024 * 1024),
        cost_estimate=NO_COST,
        name="pick",
    )(fetch_pick, panels, *after)
    return out


def gate(value, after):
    return pl.pallas_call(
        lambda *refs: None,
        out_shape=jax.ShapeDtypeStruct(value.shape, value.dtype),
        in_specs=[untouched()] * (1 + len(after)),
        out_specs=untouched(),
        input_output_aliases={0: 0},
        compiler_params=pltpu.CompilerParams(vmem_limit_bytes=1024 * 1024),
        cost_estimate=NO_COST,
        name="gate",
    )(value, *after)


def total_kernel(turns, last, stride, counts, fetch_pick, *refs):
    out, base, token, refs = *refs[-3:], list(refs[: sum(counts)])
    picks = [turn_pick(fetch_pick, turn, stride) for turn in turns]
    last_pick = turn_pick(fetch_pick, last, stride)
    token[...] = jnp.zeros_like(token)
    experts, kinds = out.shape[:2]
    grads = []
    for count in counts:
        taken, refs = refs[:count], refs[count:]
        grads.append([taken[0].at[kind] for kind in range(kinds)] if count == 1 else taken)
    for kind in range(kinds):
        terms = [grad[kind][...].astype(F32) for grad in grads]
        for e in range(experts):
            total = jnp.zeros(terms[0].shape, F32)
            for pick, term in zip(picks, terms):
                total += jnp.where(pick == e, term, 0.0)
            total = total.astype(BF16)
            out[e, kind] = total
            if e == 0:
                base[kind] = total
            else:

                @pl.when(last_pick == e)
                def _():
                    base[kind] = total


def total_pass(turns, last, stride, fetch_pick, grads, shape, after):
    counts = [len(grad) for grad in grads]
    return pl.pallas_call(
        lambda *refs: total_kernel(turns, last, stride, counts, *refs),
        out_shape=(
            jax.ShapeDtypeStruct(shape, BF16),
            jax.ShapeDtypeStruct(shape[1:], BF16),
            token_shape(),
        ),
        in_specs=[pl.BlockSpec(memory_space=pltpu.SMEM)]
        + [whole_in_vmem()] * sum(counts)
        + [untouched()] * len(after),
        out_specs=(whole_in_vmem(),) * 3,
        compiler_params=pltpu.CompilerParams(vmem_limit_bytes=VMEM_LIMIT),
        cost_estimate=NO_COST,
        name="total",
    )(fetch_pick, *[grad for slot_grads in grads for grad in slot_grads], *after)


def add_kernel(turn, stride, fetch_pick, total, base, grad, out, sums, sems):
    pick = turn_pick(fetch_pick, turn, stride)
    writes = []
    for kind in range(grad.shape[0]):
        for j, (low, high) in enumerate(spans_of(grad.shape[1])):
            here = pl.ds(low, high - low)
            sums[kind, here] = (base[kind, here].astype(F32) + grad[kind, here].astype(F32)).astype(BF16)
            write = pltpu.make_async_copy(
                sums.at[kind, here], out.at[pick, kind, here], sems.at[kind, j]
            )
            write.start()
            writes.append(write)
    for write in writes:
        write.wait()


def add_pass(turn, stride, fetch_pick, total, base, grad):
    return pl.pallas_call(
        lambda *refs: add_kernel(turn, stride, *refs),
        out_shape=jax.ShapeDtypeStruct(total.shape, BF16),
        in_specs=[pl.BlockSpec(memory_space=pltpu.SMEM), in_hbm(), whole_in_vmem(), whole_in_vmem()],
        out_specs=in_hbm(),
        input_output_aliases={1: 0},
        scratch_shapes=[pltpu.VMEM(grad.shape, BF16), pltpu.SemaphoreType.DMA((grad.shape[0], 4))],
        compiler_params=pltpu.CompilerParams(vmem_limit_bytes=12 * 1024 * 1024),
        cost_estimate=NO_COST,
        name="add",
    )(fetch_pick, total, base, grad)


def ring_step(block, order, distance):
    size = len(order)
    return lax.ppermute(
        block, "local", [(order[i], order[(i + distance) % size]) for i in range(size)]
    )


def add_rows_kernel(*refs):
    a, b, out = refs[0], refs[1], refs[-1]
    out[...] = (a[...].astype(F32) + b[...].astype(F32)).astype(out.dtype)


def add_rows(a, b, dtype, after=()):
    return pl.pallas_call(
        add_rows_kernel,
        out_shape=jax.ShapeDtypeStruct(a.shape, dtype),
        in_specs=[whole_in_vmem()] * 2 + [untouched()] * len(after),
        out_specs=whole_in_vmem(),
        compiler_params=pltpu.CompilerParams(vmem_limit_bytes=VMEM_LIMIT),
        cost_estimate=NO_COST,
        name="add_rows",
    )(a, b, *after)


def acts_kernel(turn, slots, stride, size, offsets, pieces, *refs):
    parts = len(offsets)
    x_refs, dy_refs = refs[:parts], refs[parts : 2 * parts]
    panel, (routes, weight), acts = by_kind(refs[2 * parts : 2 * parts + pieces]), refs[
        2 * parts + pieces : 2 * parts + pieces + 2
    ], refs[-1]
    units, width = panel[0].shape
    part = x_refs[0].shape[0]
    at_once = 2 if parts % 2 == 0 else 1
    slot = turn_slot(turn, slots, stride)
    for d in range(0, parts, at_once):
        here = slice(d * part, (d + at_once) * part)
        x = jnp.concatenate([ref[...] for ref in x_refs[d : d + at_once]], axis=0)
        dy = jnp.concatenate([ref[...] for ref in dy_refs[d : d + at_once]], axis=0)
        both = lax.dot_general(
            jnp.concatenate([panel[0][...], panel[1][...]], axis=0), x, CONTRACT_LAST, preferred_element_type=F32
        )
        gate, up = both[:units], both[units:]
        d_hidden = lax.dot_general(panel[2][...], dy, CONTRACT_LAST, preferred_element_type=F32)
        sources = [ring_source(size, ahead) for ahead in offsets[d : d + at_once]]
        scale = jnp.concatenate(
            [
                jnp.where(routes[pl.ds(i, 1), :] == slot, weight[pl.ds(i, 1), :], 0.0)
                for i in sources
            ],
            axis=1,
        )
        sigmoid_gate = jax.nn.sigmoid(gate)
        activated = gate * sigmoid_gate
        d_hidden = d_hidden * scale
        d_gate = d_hidden * up * sigmoid_gate * (1.0 + gate * (1.0 - sigmoid_gate))
        acts[0:units, here] = d_gate.astype(BF16)
        acts[units : 2 * units, here] = (d_hidden * activated).astype(BF16)
        acts[2 * units : 3 * units, here] = (activated * up * scale).astype(BF16)


def acts_pass(name, turn, slots, stride, offsets, x_parts, dy_parts, panel, routes, weight, after=()):
    parts = len(x_parts)
    part = x_parts[0].shape[0]
    return pl.pallas_call(
        lambda *refs: acts_kernel(
            turn, slots, stride, routes.shape[0], offsets, len(panel), *refs
        ),
        out_shape=jax.ShapeDtypeStruct((3 * panel[0].shape[-2], parts * part), BF16),
        in_specs=[whole_in_vmem()] * (2 * parts + len(panel) + 2) + [untouched()] * len(after),
        out_specs=whole_in_vmem(),
        compiler_params=pltpu.CompilerParams(vmem_limit_bytes=VMEM_LIMIT),
        cost_estimate=NO_COST,
        name=f"acts_{turn}_{name}",
    )(*x_parts, *dy_parts, *panel, routes, weight, *after)


def grads_kernel(parts, groups, kinds, *refs):
    x_refs, dy_refs = refs[:parts], refs[parts : 2 * parts]
    acts, grads = refs[2 * parts : 2 * parts + groups], refs[-kinds:]
    if kinds == 1:
        grads = [grads[0].at[kind] for kind in range(3)]
    units, width = grads[0].shape
    columns = tile_of(width, 512)
    for start in range(0, width, columns):
        here = slice(start, start + columns)
        x = jnp.concatenate([ref[:, here] for ref in x_refs], axis=0)
        dy = jnp.concatenate([ref[:, here] for ref in dy_refs], axis=0)
        d_both = jnp.concatenate([act[0 : 2 * units, :] for act in acts], axis=1)
        d_both = jnp.dot(d_both, x, preferred_element_type=F32).astype(BF16)
        grads[0][:, here] = d_both[0:units]
        grads[1][:, here] = d_both[units:]
        hidden = jnp.concatenate([act[2 * units : 3 * units, :] for act in acts], axis=1)
        grads[2][:, here] = jnp.dot(hidden, dy, preferred_element_type=F32).astype(BF16)


def grads_pass(turn, x_parts, dy_parts, acts, shapes, after=()):
    parts = len(x_parts)
    return pl.pallas_call(
        lambda *refs: grads_kernel(parts, len(acts), len(shapes), *refs),
        out_shape=tuple(jax.ShapeDtypeStruct(shape, BF16) for shape in shapes),
        in_specs=[whole_in_vmem()] * (2 * parts + len(acts)) + [untouched()] * len(after),
        out_specs=tuple(whole_in_vmem() for _ in shapes),
        compiler_params=pltpu.CompilerParams(vmem_limit_bytes=VMEM_LIMIT),
        cost_estimate=work_cost(6 * parts * acts[0].shape[0] // 3 * x_parts[0].size),
        name=f"grads_{turn}",
    )(*x_parts, *dy_parts, *acts, *after)


def chunk_kernel(wanted, slots, part, acts, panels, outs):
    units, width = panels[0][0].shape
    columns = tile_of(width, 512)

    @pl.loop(0, width // columns)
    def _(step):
        here = pl.ds(pl.multiple_of(step * columns, columns), columns)
        kinds = {"mixed": (2, 3), "grad": (0, 2)}
        sides = {
            kind: jnp.concatenate(
                [panel[which][:, here] for panel in panels for which in range(*span)], axis=0
            )
            for kind, span in kinds.items()
        }
        for out, (kind, group, row) in zip(outs, wanted):
            low, high = (units * which for which in kinds[kind])
            act = jnp.concatenate(
                [act[group][low:high, row * part : (row + 1) * part] for act in acts], axis=0
            )
            total = lax.dot_general(act, sides[kind], CONTRACT_FIRST, preferred_element_type=F32)
            out[:, here] = total.astype(BF16)


def chunk_pass(wanted, acts, panels, groups, part, cost, after=()):
    slots = len(panels)
    width = panels[0][0].shape[-1]
    pieces = [len(panel) for panel in panels]
    named = [
        (kind, g, group.index(d)) for kind, d in wanted for g, group in enumerate(groups) if d in group
    ]

    def kernel(*refs):
        act_refs = [refs[s * len(groups) : (s + 1) * len(groups)] for s in range(slots)]
        rest = refs[slots * len(groups) :]
        starts = [sum(pieces[:s]) for s in range(slots)]
        panel_refs = [by_kind(rest[a : a + n]) for a, n in zip(starts, pieces)]
        chunk_kernel(named, slots, part, act_refs, panel_refs, rest[sum(pieces) + len(after) :])

    return pl.pallas_call(
        kernel,
        out_shape=tuple(jax.ShapeDtypeStruct((part, width), BF16) for _ in wanted),
        in_specs=[whole_in_vmem()] * (slots * len(groups) + sum(pieces)) + [untouched()] * len(after),
        out_specs=tuple(whole_in_vmem() for _ in wanted),
        compiler_params=pltpu.CompilerParams(vmem_limit_bytes=VMEM_LIMIT),
        cost_estimate=cost,
        name=f"chunks_{len(wanted)}",
    )(*[act for slot_acts in acts for act in slot_acts], *[piece for panel in panels for piece in panel], *after)


def final_rows_kernel(*refs):
    a, b, out, token = refs[0], refs[1], *refs[-2:]
    out[...] = (a[...].astype(F32) + b[...]).astype(out.dtype)
    token[...] = jnp.zeros_like(token)


def final_rows(a, b, cost, after):
    return pl.pallas_call(
        final_rows_kernel,
        out_shape=(jax.ShapeDtypeStruct(a.shape, BF16), token_shape()),
        in_specs=[whole_in_vmem()] * 2 + [untouched()] * len(after),
        out_specs=(whole_in_vmem(), whole_in_vmem()),
        compiler_params=pltpu.CompilerParams(vmem_limit_bytes=VMEM_LIMIT),
        cost_estimate=cost,
        name="final_rows",
    )(a, b, *after)


class Line:
    def __init__(self):
        self.tail = ()

    def step(self, make):
        out = make(self.tail)
        self.tail = (out[-1] if isinstance(out, (tuple, list)) else out,)
        return out

    def arrive(self, value):
        return self.step(lambda after: gate(value, after))


def body(tokens, cotangent, routes, route_weight, fetch_pick, panels):
    panels = pltpu.with_memory_space_constraint(panels, pltpu.HBM)
    fetch_pick_far = pltpu.with_memory_space_constraint(fetch_pick, pltpu.HBM)
    slots = fetch_pick.shape[1]
    stride = lax.axis_size("node") // slots
    part, width = tokens.shape
    order = ring_order(lax.axis_size("local"))
    size = len(order)
    up_most, down_most = size // 2, size - 1 - size // 2
    last, late = slots - 1, slots - 2
    middle = list(range(1, late))
    line = Line()

    ring_routes = routes.reshape(size, part)
    ring_weight = route_weight.reshape(size, part)
    near = [d for d in range(size) if min(d, size - d) <= size // 4 and d != size // 4]
    groups = [near, [d for d in range(size) if d not in near]]
    rows = [d for group in groups for d in group]
    x_parts = [tokens] + [None] * (size - 1)
    dy_parts = [cotangent] + [None] * (size - 1)
    acts = [[None, None] for _ in range(slots)]
    grads, back = [None] * slots, [None] * slots

    def make_acts(turn, g):
        take = groups[g]
        acts[turn][g] = line.step(
            lambda after: acts_pass(
                "nf"[g],
                turn,
                slots,
                stride,
                take,
                [x_parts[d] for d in take],
                [dy_parts[d] for d in take],
                read[turn],
                ring_routes,
                ring_weight,
                after,
            )
        )

    def make_grads(turn):
        shape = panels.shape[1:]
        grads[turn] = line.step(
            lambda after: grads_pass(
                turn,
                [x_parts[d] for d in rows],
                [dy_parts[d] for d in rows],
                acts[turn],
                [shape[1:]] * shape[0] if turn in middle else [shape],
                after,
            )
        )
        if turn != last:
            back[turn] = [exchange(grad, turn, slots) if turn else grad for grad in grads[turn]]

    read = [None] * slots
    picked = line.step(lambda after: pick_pass([late], stride, fetch_pick_far, panels, False, after))
    read[late] = [exchange(picked[0], late, slots)]
    for turn in middle:
        picked = line.step(lambda after: pick_pass([turn], stride, fetch_pick, panels, True, after))
        read[turn] = [exchange(piece, turn, slots) for piece in picked]
    picked = line.step(lambda after: pick_pass([last, 0], stride, fetch_pick, panels, False, after))
    read[last], read[0] = [[piece] for piece in picked]

    chains = [(x_parts, 1, up_most), (dy_parts, -1, up_most), (x_parts, -1, down_most), (dy_parts, 1, down_most)]
    moving = [ring_step(parts[0], order, way) for parts, way, _ in chains]
    for turn in middle:
        read[turn] = [line.arrive(piece) for piece in read[turn]]
    for hop in range(1, up_most + 1):
        for i, (parts, way, hops) in enumerate(chains):
            if hop > hops:
                continue
            if hop == max(1, up_most // 2) and i == 2:
                read[late] = [line.arrive(read[late][0])]
                read[last] = [exchange(line.arrive(read[last][0]), last, slots)]
            arrived = line.arrive(moving[i])
            parts[-way * hop % size] = arrived
            if hop < hops:
                moving[i] = ring_step(arrived, order, way)
            if hop == max(1, up_most // 2) and i == len(chains) - 1:
                for turn in middle + [0, late]:
                    make_acts(turn, 0)

    make_acts(late, 1)
    make_grads(late)
    for turn in middle:
        make_acts(turn, 1)
        make_grads(turn)
    make_acts(0, 1)
    read[last] = [line.arrive(read[last][0])]
    make_acts(last, 1)
    make_acts(last, 0)
    for turn in middle:
        back[turn] = [line.arrive(grad) for grad in back[turn]]

    kinds = ("mixed", "grad")
    early = [("mixed", up_most), ("grad", size - up_most), ("mixed", size - down_most), ("grad", down_most)]
    early_cost = work_cost(6 * len(early) * slots * part * read[0][0].size // 6)
    later = [(kind, d) for kind in kinds for d in range(size) if (kind, d) not in early]
    chunks = dict(zip(early, line.step(lambda after: chunk_pass(early, acts, read, groups, part, early_cost, after))))
    chains = [("mixed", 1, up_most), ("grad", -1, up_most), ("mixed", -1, down_most), ("grad", 1, down_most)]
    moving = [ring_step(chunks[kind, way * hops % size], order, way) for kind, way, hops in chains]
    chunks.update(zip(later, line.step(lambda after: chunk_pass(later, acts, read, groups, part, NO_COST, after))))
    make_grads(last)
    make_grads(0)

    sums = {}
    for hop in range(1, up_most + 1):
        for i, (kind, way, hops) in enumerate(chains):
            if hop > hops:
                continue
            if hop == max(1, up_most // 2) and i == 2:
                back[late] = [line.arrive(back[late][0])]
                back[last] = exchange(line.arrive(grads[last][0]), last, slots)
            left = hops - hop
            if left:
                chunk = chunks[kind, way * left % size]
                arrived = line.step(lambda after: add_rows(moving[i], chunk, BF16, after))
                moving[i] = ring_step(arrived, order, way)
            elif kind not in sums:
                sums[kind] = line.step(lambda after: add_rows(moving[i], chunks[kind, 0], F32, after))
                if len(sums) == 2:
                    panel_grad, base, _ = line.step(
                        lambda after: total_pass(
                            list(range(last)), last, stride, fetch_pick, back[:last], panels.shape, after
                        )
                    )
            else:
                cost = work_cost(LAST_FLOPS) if (kind, hop) == (chains[1][0], up_most) else NO_COST
                sums[kind], _ = line.step(lambda after: final_rows(moving[i], sums[kind], cost, after))
    back[last] = line.arrive(back[last])
    panel_grad = add_pass(last, stride, fetch_pick, panel_grad, base, back[last])
    return sums["mixed"], sums["grad"], panel_grad


def solution(mesh):
    return jax.shard_map(
        body,
        mesh=mesh,
        in_specs=(
            P(("node", "local"), None),
            P(("node", "local"), None),
            P("node", None),
            P("node", None),
            P(),
            P("node", None, "local", None),
        ),
        out_specs=(
            P(("node", "local"), None),
            P(("node", "local"), None),
            P("node", None, "local", None),
        ),
        check_vma=False,
    )
```
